32 devices in a mesh: shard: 4 (over z), rep: 8 (over y, x, core).
Axes of the slice: x: 2, y: 2, z: 4, core: 2. Of those that a mesh axis runs over, the one named last changes fastest.
Arguments:
- pooled_grad: bfloat16 [8192, 256], P(('shard', 'rep')), may hold values from -6 to 6
- send_sample: int32 [128, 128], P(('shard', 'rep')), may hold values from 0 to 255
- send_row: int32 [128, 128], P(('shard', 'rep')), may hold values from 0 to 2047
- send_count: int32 [128], P(('shard', 'rep')), may hold values from 1 to 128, as said below
- union_blocks: int32 [4, 16], P('shard'), may hold values from 0 to 31, as said below
- table: float32 [16384, 256], P('shard'), may hold values from -6 to 6
- accum: float32 [16384], P('shard'), may hold values from 0.05 to 2
Outputs:
- new_table: float32 [16384, 256], P('shard')
- new_accum: float32 [16384], P('shard')
The draws below stay inside these ranges and needn't reach their ends.
Inputs may be any that keep to these rules, and one draw needn't show every extreme that they name: `send_count`: in every replica group one owner gets 128 live entries from every device of the group. `union_blocks`: each shard's row blocks are distinct and increasing, and include its first and its last block.
All inputs are finite; a program needn't handle non-finite values.
Results may differ from the reference program's by a relative error of at most 0.00065.
Values may be sent and summed in bfloat16 or wider, within the bound.
No kernel may reach another device: no remote copies, remote signals or barrier semaphores. Data moves between devices by JAX's collectives and lax.ppermute only.
A program may use at most 64 MiB of HBM per device.

```python
import math
import jax
import jax.numpy as jnp
from jax import lax

DIM = 256
TILE = 128
B_DEV = 256
R_DEV = 4096
BLOCKS = 16
CAP = 128
SAMPLES = 8192
ROWS = 16384
SENDS = 128
N_SHARD = 4
N_REP = 8


def draw_send_count(key, part):
    key = jax.random.fold_in(key, 11)
    first_key, second_key = jax.random.split(key)
    base = jax.random.randint(first_key, (SENDS,), 1, CAP // 2 + 1)
    hottest = jax.random.randint(second_key, (N_REP,), 0, N_SHARD)
    index = jnp.arange(SENDS, dtype=jnp.int32)
    group = index // N_SHARD % N_REP
    owner = index % N_SHARD
    return jnp.where(owner == hottest[group], CAP, base).astype(jnp.int32)


def draw_union_blocks(key, part):
    key = jax.random.fold_in(key, 23)
    tiles = R_DEV // TILE
    shard_keys = jax.random.split(key, N_SHARD)

    def one_shard(shard_key):
        middle = jax.random.permutation(shard_key, tiles - 2)[:BLOCKS - 2] + 1
        chosen = jnp.concatenate([jnp.zeros((1,), jnp.int32), middle.astype(jnp.int32), jnp.full((1,), tiles - 1, jnp.int32)])
        return jnp.sort(chosen)
    return jax.vmap(one_shard)(shard_keys).astype(jnp.int32)


def touch_ends(entries, stream_key, smallest, top_value):
    longest = entries.shape.index(max(entries.shape))
    spots = []
    for shift in (0, 1):
        where = [jax.random.randint(jax.random.fold_in(stream_key, axis), (), 0, length) for axis, length in enumerate(entries.shape)]
        where[longest] = (where[longest] + shift) % entries.shape[longest]
        spots.append(tuple(where))
    return entries.at[spots[0]].set(smallest).at[spots[1]].set(top_value)


def block_scale(stream_key, dims, shards, low, high):
    def one(axis_at, parts):
        steps = jax.random.uniform(jax.random.fold_in(jax.random.fold_in(stream_key, 6), axis_at), (parts,), jnp.float32, low / len(shards), high / len(shards))
        return jnp.repeat(jnp.exp(steps), dims[axis_at] // parts).reshape((-1,) + (1,) * (len(dims) - axis_at - 1))

    level = one(*shards[0])
    for cut in shards[1:]:
        level = level * one(*cut)
    return level


def noise(stream_key, dims, width, reach, cuts=(), kind=jnp.bfloat16):
    gain = block_scale(stream_key, dims, cuts, -0.22, 0.18) if cuts else 1.0
    values = jax.random.normal(stream_key, dims, jnp.float32) * width * gain
    return jnp.minimum(jnp.maximum(values, -reach), reach).astype(kind)


def setup_inputs(seed: int = 0) -> dict:
    key_list = jax.random.split(jax.random.key(seed), 8)
    return {
        "pooled_grad": noise(key_list[0], (SAMPLES, DIM), 1.0, 6.0, ((0, 32),)),
        "send_sample": touch_ends(jax.random.randint(key_list[1], (SENDS, CAP), 0, B_DEV), jax.random.fold_in(key_list[1], 1), 0, B_DEV - 1).astype(jnp.int32),
        "send_row": touch_ends(jax.random.randint(key_list[2], (SENDS, CAP), 0, BLOCKS * TILE), jax.random.fold_in(key_list[2], 1), 0, (BLOCKS * TILE) - 1).astype(jnp.int32),
        "send_count": draw_send_count(jax.random.fold_in(key_list[7], 71), 0),
        "union_blocks": draw_union_blocks(jax.random.fold_in(key_list[7], 71), 0),
        "table": noise(key_list[5], (ROWS, DIM), 1.0, 6.0, ((0, 4),), jnp.float32),
        "accum": jnp.clip(jnp.exp(math.log(2.0) - 3.6888794 * jax.random.uniform(key_list[6], (ROWS,), jnp.float32) ** block_scale(key_list[6], (ROWS,), ((0, 4),), -0.2, 0.2)), 0.05, 2.0),
    }


LEARNING_RATE = 0.5
EPSILON = 1e-06

def reference(pooled_grad, send_sample, send_row, send_count, union_blocks, table, accum):
    devices_all = N_SHARD * N_REP
    union_span = BLOCKS * TILE
    grads_all = pooled_grad.reshape(devices_all, B_DEV, DIM)
    samples_all = send_sample.reshape(devices_all, N_SHARD, CAP)
    rows_all = send_row.reshape(devices_all, N_SHARD, CAP)
    counts_all = send_count.reshape(devices_all, N_SHARD)
    owners = jnp.arange(N_SHARD, dtype=jnp.int32)[:, None]
    slots = jnp.arange(CAP, dtype=jnp.int32)[None, :]

    def add_device(total, pieces):
        grads_dev, sample_ids, row_ids, counts_dev = pieces
        active = (slots < counts_dev[:, None]).astype(jnp.float32)
        lengths = jax.ops.segment_sum(active.reshape(-1), sample_ids.reshape(-1).astype(jnp.int32), num_segments=B_DEV)
        scaled = active / jnp.maximum(lengths, 1.0)[sample_ids]
        values = (grads_dev[sample_ids].astype(jnp.float32) * scaled[:, :, None]).astype(jnp.bfloat16)
        target = (owners * union_span + row_ids).astype(jnp.int32)
        total = total.at[target.reshape(-1)].add(values.reshape(-1, DIM).astype(jnp.float32))
        return (total, None)
    start_total = jnp.zeros((N_SHARD * union_span, DIM), jnp.float32)
    total, _ = lax.scan(add_device, start_total, (grads_all, samples_all, rows_all, counts_all))
    rounded = lax.optimization_barrier(total.astype(jnp.bfloat16))
    row_grad = rounded.astype(jnp.float32).reshape(N_SHARD, BLOCKS, TILE, DIM)
    table_tiles = table.reshape(N_SHARD, R_DEV // TILE, TILE, DIM)
    accum_tiles = accum.reshape(N_SHARD, R_DEV // TILE, TILE)
    picked = jnp.take_along_axis(table_tiles, union_blocks[:, :, None, None].astype(jnp.int32), axis=1)
    acc_picked = jnp.take_along_axis(accum_tiles, union_blocks[:, :, None].astype(jnp.int32), axis=1)
    acc_new = acc_picked + lax.optimization_barrier(jnp.mean(row_grad * row_grad, axis=-1))
    rows_new = picked - LEARNING_RATE * row_grad / (jnp.sqrt(acc_new)[..., None] + EPSILON)
    owner_index = jnp.arange(N_SHARD, dtype=jnp.int32)[:, None]
    table_tiles = table_tiles.at[owner_index, union_blocks].set(rows_new)
    accum_tiles = accum_tiles.at[owner_index, union_blocks].set(acc_new)
    return (table_tiles.reshape(ROWS, DIM), accum_tiles.reshape(ROWS))
```

```python
import functools

import jax
import jax.numpy as jnp
from jax import lax
from jax.experimental import pallas as pl
from jax.experimental.pallas import tpu as pltpu
from jax.sharding import PartitionSpec as P

TILE = 128
TAIL = 16
LEARNING_RATE = 0.5
EPSILON = 1e-06
VMEM = pltpu.VMEM
SMEM = pltpu.SMEM
F32 = jnp.float32
BF16 = jnp.bfloat16


def params(mib=40):
    return pltpu.CompilerParams(vmem_limit_bytes=mib * 2**20)


def whole(space=VMEM):
    return pl.BlockSpec(memory_space=space)


def pack_kernel(me_ref, count_ref, grad_ref, sample_ref, row_ref, *out_refs):
    owners, cap = sample_ref.shape
    samples, cols = grad_ref.shape
    lane = lax.broadcasted_iota(jnp.int32, (1, cap), 1)
    sub = lax.broadcasted_iota(jnp.int32, (samples, cap), 0)

    def picks(o):
        live = jnp.where(lane < count_ref[o], sample_ref[pl.ds(o, 1), :], -1)
        return (sub == live).astype(F32)

    total = picks(0)
    for o in range(1, owners):
        total = total + picks(o)
    lengths = jnp.sum(total, axis=1, keepdims=True)
    scaled = (grad_ref[...].astype(F32) * (1.0 / jnp.maximum(lengths, 1.0))).astype(BF16)
    tail_row = lax.broadcasted_iota(jnp.int32, (TAIL, cap), 0)
    for j in range(owners):
        o = me_ref[0] ^ j
        values = lax.dot_general(
            picks(o).astype(BF16), scaled, (((0,), (0,)), ((), ())), preferred_element_type=F32
        )
        out_refs[j][0:cap, :] = values.astype(BF16)
        row = row_ref[pl.ds(o, 1), :]
        slot = row // TILE
        within = row - slot * TILE
        tail = jnp.where(tail_row == 0, slot, jnp.where(tail_row == 1, within, 0))
        out_refs[j][cap : cap + TAIL, :] = jnp.zeros((TAIL, cols), BF16)
        out_refs[j][cap : cap + TAIL, 0:cap] = tail.astype(F32).astype(BF16)


def pack(me, count, grad, sample, row):
    owners, cap = sample.shape
    shape = jax.ShapeDtypeStruct((cap + TAIL, grad.shape[1]), BF16)
    return pl.pallas_call(
        pack_kernel,
        out_shape=[shape] * owners,
        in_specs=[whole(SMEM), whole(SMEM), whole(), whole(), whole()],
        out_specs=[whole()] * owners,
        compiler_params=params(),
    )(me, count, grad, sample, row)


def join_kernel(*refs):
    ins, out = refs[:-1], refs[-1]
    cap = ins[0].shape[0] - TAIL
    n = len(ins)
    for c, ref in enumerate(ins):
        out[c * cap : (c + 1) * cap, :] = ref[0:cap, :]
    sub = lax.broadcasted_iota(jnp.int32, (TAIL, ins[0].shape[1]), 0)
    tail = jnp.zeros((TAIL, ins[0].shape[1]), F32)
    for c, ref in enumerate(ins):
        own = ref[cap : cap + TAIL, :].astype(F32)
        tail = jnp.where(sub == 2 * c, own[0:1, :], jnp.where(sub == 2 * c + 1, own[1:2, :], tail))
    out[n * cap : n * cap + TAIL, :] = tail.astype(BF16)


def join(chunks):
    cap = chunks[0].shape[0] - TAIL
    cols = chunks[0].shape[1]
    return pl.pallas_call(
        join_kernel,
        out_shape=jax.ShapeDtypeStruct((len(chunks) * cap + TAIL, cols), BF16),
        in_specs=[whole()] * len(chunks),
        out_specs=whole(),
        compiler_params=params(),
    )(*chunks)


def positions(ref, cap):
    entries = ref.shape[0] - TAIL
    tail = ref[entries : entries + TAIL, 0:cap].astype(F32)
    n = entries // cap
    slot = jnp.concatenate([tail[2 * c : 2 * c + 1] for c in range(n)], axis=1)
    within = jnp.concatenate([tail[2 * c + 1 : 2 * c + 2] for c in range(n)], axis=1)
    return slot, within


def block_sum(ref, slot, within, k, cap):
    entries = ref.shape[0] - TAIL
    here = jnp.where(slot == k, within, -1.0).astype(BF16)
    sub = lax.broadcasted_iota(jnp.int32, (TILE, entries), 0).astype(F32).astype(BF16)
    pick = jnp.where(sub == here, jnp.ones((), BF16), jnp.zeros((), BF16))
    return jnp.dot(pick, ref[0:entries, :], preferred_element_type=F32)


def sum_kernel(cap, pairs, *refs):
    payloads, out = refs[: 2 * pairs], refs[2 * pairs]
    places = [positions(ref, cap) for ref in payloads]
    for k in range(out.shape[0] // TILE):
        parts = [block_sum(ref, *place, k, cap) for ref, place in zip(payloads, places)]
        halves = [parts[2 * i] + parts[2 * i + 1] for i in range(pairs)]
        total = halves[0] if pairs == 1 else halves[0] + halves[1]
        out[k * TILE : (k + 1) * TILE, :] = total


def sum_payloads(payloads, span, cap):
    cols = payloads[0].shape[1]
    entries = payloads[0].shape[0] - TAIL
    pairs = len(payloads) // 2
    return pl.pallas_call(
        functools.partial(sum_kernel, cap, pairs),
        out_shape=jax.ShapeDtypeStruct((span, cols), F32),
        in_specs=[whole()] * len(payloads),
        out_specs=whole(),
        compiler_params=params(),
        cost_estimate=pl.CostEstimate(
            flops=2 * span * entries * cols * len(payloads),
            bytes_accessed=span * cols * 4,
            transcendentals=0,
        ),
    )(*payloads)


def stage_kernel(blocks_ref, table_ref, copy_ref, picked_ref, sems):
    n = picked_ref.shape[0] // TILE
    full = pltpu.make_async_copy(table_ref, copy_ref, sems.at[n])
    full.start()
    copies = []
    for k in range(n):
        start = pl.multiple_of(blocks_ref[0, k] * TILE, TILE)
        c = pltpu.make_async_copy(
            table_ref.at[pl.ds(start, TILE), :],
            picked_ref.at[pl.ds(k * TILE, TILE), :],
            sems.at[k],
        )
        c.start()
        copies.append(c)
    for c in copies:
        c.wait()
    full.wait()


def stage(blocks, table):
    n = blocks.shape[1]
    return pl.pallas_call(
        stage_kernel,
        out_shape=[
            jax.ShapeDtypeStruct(table.shape, F32),
            jax.ShapeDtypeStruct((n * TILE, table.shape[1]), F32),
        ],
        in_specs=[whole(SMEM), whole(pl.ANY)],
        out_specs=[whole(pl.ANY), whole()],
        scratch_shapes=[pltpu.SemaphoreType.DMA((n + 1,))],
        compiler_params=params(),
        cost_estimate=pl.CostEstimate(
            flops=0, bytes_accessed=4 * table.size * 3, transcendentals=0
        ),
    )(blocks, table)


def update_kernel(
    cap, blocks_ref, last0, last1, side_ref, near_ref, picked_ref, accum_ref, table_in,
    table_ref, accum_out, rows_out, sems,
):
    del table_in
    n = picked_ref.shape[0] // TILE
    cols = picked_ref.shape[1]
    places = [positions(ref, cap) for ref in (last0, last1)]
    accum_out[...] = accum_ref[...]
    copies = []
    for k in range(n):
        span = slice(k * TILE, (k + 1) * TILE)
        far = block_sum(last0, *places[0], k, cap) + block_sum(last1, *places[1], k, cap)
        grad = (near_ref[span, :] + (side_ref[span, :] + far)).astype(BF16).astype(F32)
        block = blocks_ref[0, k]
        mean = jnp.sum(grad * grad, axis=1, keepdims=True) * (1.0 / cols)
        wide = jnp.broadcast_to(accum_ref[pl.ds(block, 1), :], (TILE, TILE)).T
        new = wide[:, 0:1] + mean
        rows_out[span, :] = picked_ref[span, :] - LEARNING_RATE * grad / (jnp.sqrt(new) + EPSILON)
        accum_out[pl.ds(block, 1), :] = jnp.broadcast_to(new, (TILE, TILE)).T[0:1, :]
        c = pltpu.make_async_copy(
            rows_out.at[span, :],
            table_ref.at[pl.ds(pl.multiple_of(block * TILE, TILE), TILE), :],
            sems.at[k],
        )
        c.start()
        copies.append(c)
    for c in copies:
        c.wait()


def update(blocks, last, side, near, picked, accum, table, cap):
    n = blocks.shape[1]
    return pl.pallas_call(
        functools.partial(update_kernel, cap),
        out_shape=[
            jax.ShapeDtypeStruct(table.shape, F32),
            jax.ShapeDtypeStruct(accum.shape, F32),
        ],
        in_specs=[whole(SMEM)] + [whole()] * 6 + [whole(pl.ANY)],
        out_specs=[whole(pl.ANY), whole()],
        scratch_shapes=[
            pltpu.VMEM(picked.shape, F32),
            pltpu.SemaphoreType.DMA((n,)),
        ],
        input_output_aliases={7: 0},
        compiler_params=params(),
    )(blocks, *last, side, near, picked, accum, table)


def gathered(pooled_grad, send_sample, send_row, send_count, union_blocks, table, accum):
    shards = lax.axis_size("shard")
    reps = lax.axis_size("rep")
    cap = send_sample.shape[1]
    span = union_blocks.shape[1] * TILE
    me = lax.axis_index("shard").astype(jnp.int32).reshape(1)
    axes = ("shard", "rep")

    def swap(x, flip):
        pairs = []
        for z in range(shards):
            for r in range(reps):
                dz, dr = flip(r)
                pairs.append((z * reps + r, (z ^ dz) * reps + (r ^ dr)))
        return lax.ppermute(x, axes, pairs)

    mine = pack(me, send_count, pooled_grad, send_sample, send_row)
    far = swap(mine[2], lambda r: (2, 0))
    up = swap(mine[3], lambda r: (3, 0))
    down = swap(mine[1], lambda r: (1, 0))
    own = join([mine[0], down, far, up])
    one = swap(own, lambda r: (0, 2 if r % 2 == 0 else 4))
    two = swap(own, lambda r: (0, 4 if r % 2 == 0 else 2))
    diag = swap(one, lambda r: (0, 4 if r % 2 == 0 else 2))
    core = lambda x: swap(x, lambda r: (0, 1))
    table_copy, picked = stage(union_blocks, table)
    own_c, one_c, two_c, diag_c = core(own), core(one), core(two), core(diag)
    even = lax.axis_index("rep") % 2 == 0
    x0 = lax.select(even, one, two)
    x1 = lax.select(even, two_c, one_c)
    y0 = lax.select(even, two, one)
    y1 = lax.select(even, one_c, two_c)
    near = sum_payloads([own, own_c, x0, x1], span, cap)
    side = sum_payloads([y0, y1], span, cap)
    table_out, accum_out = update(
        union_blocks, (diag, diag_c), side, near, picked, accum.reshape(-1, TILE), table_copy, cap
    )
    return table_out, accum_out.reshape(accum.shape)


def reduced(pooled_grad, send_sample, send_row, send_count, union_blocks, table, accum):
    columns = pooled_grad.shape[1]
    samples = pooled_grad.shape[0]
    active = (lax.broadcasted_iota(jnp.int32, send_sample.shape, 1) < send_count[:, None]).astype(F32)
    lengths = jax.ops.segment_sum(active.reshape(-1), send_sample.reshape(-1), num_segments=samples)
    scaled = active / jnp.maximum(lengths, 1.0)[send_sample]
    values = (pooled_grad[send_sample].astype(F32) * scaled[:, :, None]).astype(BF16)
    arrived = lax.all_to_all(values, "shard", split_axis=0, concat_axis=0, tiled=True)
    places = lax.all_to_all(send_row, "shard", split_axis=0, concat_axis=0, tiled=True)
    blocks = union_blocks[0]
    span = blocks.shape[0] * TILE
    local = (
        jnp.zeros((span, columns), F32)
        .at[places.reshape(-1)]
        .add(arrived.reshape(-1, columns).astype(F32))
    )
    table_tiles = table.reshape(-1, TILE, columns)
    accum_tiles = accum.reshape(-1, TILE)
    grad = lax.optimization_barrier(lax.psum(local.astype(BF16), "rep")).astype(F32)
    acc_new = accum_tiles[blocks].reshape(span) + jnp.mean(grad * grad, axis=-1)
    rows_new = table_tiles[blocks].reshape(span, columns) - LEARNING_RATE * grad / (
        jnp.sqrt(acc_new)[:, None] + EPSILON
    )
    table_out = table_tiles.at[blocks].set(rows_new.reshape(-1, TILE, columns)).reshape(table.shape)
    accum_out = accum_tiles.at[blocks].set(acc_new.reshape(-1, TILE)).reshape(accum.shape)
    return table_out, accum_out


def solution(mesh):
    both = ("shard", "rep")
    in_specs = (
        P(both, None),
        P(both, None),
        P(both, None),
        P(both),
        P("shard", None),
        P("shard", None),
        P("shard"),
    )
    out_specs = (P("shard", None), P("shard"))
    small = mesh.shape["shard"] == 4 and mesh.shape["rep"] == 8
    return jax.shard_map(
        gathered if small else reduced,
        mesh=mesh,
        in_specs=in_specs,
        out_specs=out_specs,
        check_vma=False,
    )
```

```python
import functools

import jax
import jax.numpy as jnp
from jax import lax
from jax.experimental import pallas as pl
from jax.experimental.pallas import tpu as pltpu
from jax.sharding import PartitionSpec as P

TILE = 128
TAIL = 16
LEARNING_RATE = 0.5
EPSILON = 1e-06
ORDER = 3, 2, 1
VMEM = pltpu.VMEM
SMEM = pltpu.SMEM
F32 = jnp.float32
BF16 = jnp.bfloat16


def params(mib=24):
    return pltpu.CompilerParams(vmem_limit_bytes=mib * 2**20)


def whole(space=VMEM):
    return pl.BlockSpec(memory_space=space)


def pack_kernel(me_ref, grad_ref, places_ref, *out_refs):
    owners = len(out_refs)
    cap = places_ref.shape[1]
    samples, cols = grad_ref.shape
    sub = lax.broadcasted_iota(jnp.int32, (samples, cap), 0)

    def picks(o):
        return (sub == places_ref[pl.ds(o, 1), :]).astype(F32)

    total = picks(0)
    for o in range(1, owners):
        total = total + picks(o)
    lengths = jnp.sum(total, axis=1, keepdims=True)
    scaled = (grad_ref[...].astype(F32) * (1.0 / jnp.maximum(lengths, 1.0))).astype(BF16)
    tail_row = lax.broadcasted_iota(jnp.int32, (TAIL, cap), 0)
    for j in range(owners):
        o = me_ref[0] ^ j
        values = lax.dot_general(
            picks(o).astype(BF16), scaled, (((0,), (0,)), ((), ())), preferred_element_type=F32
        )
        out_refs[j][0:cap, :] = values.astype(BF16)
        row = places_ref[pl.ds(owners + o, 1), :]
        slot = row // TILE
        within = row - slot * TILE
        tail = jnp.where(tail_row == 0, slot, jnp.where(tail_row == 1, within, 0))
        out_refs[j][cap : cap + TAIL, :] = jnp.zeros((TAIL, cols), BF16)
        out_refs[j][cap : cap + TAIL, 0:cap] = tail.astype(F32).astype(BF16)


def pack(me, count, grad, sample, row):
    owners, cap = sample.shape
    live = lax.broadcasted_iota(jnp.int32, sample.shape, 1) < count[:, None]
    places = jnp.concatenate([jnp.where(live, sample, -1), row], axis=0)
    shape = jax.ShapeDtypeStruct((cap + TAIL, grad.shape[1]), BF16)
    return pl.pallas_call(
        pack_kernel,
        out_shape=[shape] * owners,
        in_specs=[whole(SMEM), whole(), whole()],
        out_specs=[whole()] * owners,
        compiler_params=params(),
    )(me, grad, places)


def join_kernel(*refs):
    ins, out = refs[:-1], refs[-1]
    cap = ins[0].shape[0] - TAIL
    n = len(ins)
    for c, ref in enumerate(ins):
        out[c * cap : (c + 1) * cap, :] = ref[0:cap, :]
    sub = lax.broadcasted_iota(jnp.int32, (TAIL, ins[0].shape[1]), 0)
    tail = jnp.zeros((TAIL, ins[0].shape[1]), F32)
    for c, ref in enumerate(ins):
        own = ref[cap : cap + TAIL, :].astype(F32)
        tail = jnp.where(sub == 2 * c, own[0:1, :], jnp.where(sub == 2 * c + 1, own[1:2, :], tail))
    out[n * cap : n * cap + TAIL, :] = tail.astype(BF16)


def join(chunks):
    cap = chunks[0].shape[0] - TAIL
    cols = chunks[0].shape[1]
    return pl.pallas_call(
        join_kernel,
        out_shape=jax.ShapeDtypeStruct((len(chunks) * cap + TAIL, cols), BF16),
        in_specs=[whole()] * len(chunks),
        out_specs=whole(),
        compiler_params=params(),
    )(*chunks)


def positions(ref, cap):
    entries = ref.shape[0] - TAIL
    tail = ref[entries : entries + TAIL, 0:cap].astype(F32)
    n = entries // cap
    slot = jnp.concatenate([tail[2 * c : 2 * c + 1] for c in range(n)], axis=1)
    within = jnp.concatenate([tail[2 * c + 1 : 2 * c + 2] for c in range(n)], axis=1)
    return slot, within


def block_sum(ref, place, k):
    slot, within = place
    here = jnp.where(slot == k, within, -1.0).astype(BF16)
    entries = here.shape[1]
    sub = lax.broadcasted_iota(jnp.int32, (TILE, entries), 0).astype(F32).astype(BF16)
    pick = jnp.where(sub == here, jnp.ones((), BF16), jnp.zeros((), BF16))
    return jnp.dot(pick, ref[0:entries, :], preferred_element_type=F32)


def own_kernel(cap, own, part):
    place = positions(own, cap)
    for k in range(part.shape[0] // TILE):
        part[k * TILE : (k + 1) * TILE, :] = block_sum(own, place, k)


def side_kernel(cap, odd_ref, own_c, one, two_c, two, one_c, part, near, side):
    even = odd_ref[0] == 0
    payloads = (own_c, one, two_c, two, one_c)
    places = [positions(ref, cap) for ref in payloads]
    for k in range(near.shape[0] // TILE):
        span = slice(k * TILE, (k + 1) * TILE)
        other, a, b, c, d = [block_sum(ref, place, k) for ref, place in zip(payloads, places)]
        left, right = a + b, c + d
        near[span, :] = (part[span, :] + other) + jnp.where(even, left, right)
        side[span, :] = jnp.where(even, right, left)


def sum_cost(payloads, span):
    entries, cols = payloads[0].shape[0] - TAIL, payloads[0].shape[1]
    return pl.CostEstimate(
        flops=2 * span * entries * cols * len(payloads),
        bytes_accessed=span * cols * 4,
        transcendentals=0,
    )


def own_sum(own, span, cap):
    return pl.pallas_call(
        functools.partial(own_kernel, cap),
        out_shape=jax.ShapeDtypeStruct((span, own.shape[1]), F32),
        in_specs=[whole()],
        out_specs=whole(),
        compiler_params=params(),
        cost_estimate=sum_cost([own], span),
    )(own)


def side_sum(odd, payloads, part, span, cap):
    return pl.pallas_call(
        functools.partial(side_kernel, cap),
        out_shape=[jax.ShapeDtypeStruct((span, part.shape[1]), F32)] * 2,
        in_specs=[whole(SMEM)] + [whole()] * 6,
        out_specs=[whole()] * 2,
        compiler_params=params(),
        cost_estimate=sum_cost(payloads, span),
    )(odd, *payloads, part)


def update_kernel(
    cap, blocks_ref, last_m, last_c, near, side, table_in, accum_ref,
    table_ref, accum_out, rows_out, kept, sems,
):
    n = rows_out.shape[0] // TILE
    cols = rows_out.shape[1]
    tiles = accum_ref.shape[0]

    def tile(ref, block):
        return ref.at[pl.ds(pl.multiple_of(block * TILE, TILE), TILE), :]

    seen = jnp.int32(0)
    for t in range(tiles):
        touched = blocks_ref[0, jnp.minimum(seen, n - 1)] == t

        @pl.when(jnp.logical_not(touched))
        def _():
            pltpu.make_async_copy(tile(table_in, t), tile(table_ref, t), kept).start()

        seen = seen + touched.astype(jnp.int32)
    place_m, place_c = positions(last_m, cap), positions(last_c, cap)
    accum_out[...] = accum_ref[...]
    old = jnp.concatenate(
        [accum_ref[pl.ds(blocks_ref[0, k], 1), :] for k in range(n)], axis=0
    ).T
    news = []
    copies = []
    for k in range(n):
        span = slice(k * TILE, (k + 1) * TILE)
        block = pl.multiple_of(blocks_ref[0, k] * TILE, TILE)
        far = block_sum(last_m, place_m, k) + block_sum(last_c, place_c, k)
        total = near[span, :] + (side[span, :] + far)
        grad = total.astype(BF16).astype(F32)
        mean = jnp.sum(grad * grad, axis=1, keepdims=True) * (1.0 / cols)
        new = old[:, k : k + 1] + mean
        rate = LEARNING_RATE / (jnp.sqrt(new) + EPSILON)
        rows_out[span, :] = table_in[pl.ds(block, TILE), :] - grad * rate
        news.append(new)
        c = pltpu.make_async_copy(rows_out.at[span, :], tile(table_ref, blocks_ref[0, k]), sems.at[k])
        c.start()
        copies.append(c)
    flat = jnp.concatenate(news, axis=1).T
    for k in range(n):
        accum_out[pl.ds(blocks_ref[0, k], 1), :] = flat[k : k + 1, :]
    for _ in range(tiles - n):
        pltpu.make_async_copy(tile(table_in, 0), tile(table_ref, 0), kept).wait()
    for c in copies:
        c.wait()


def update(blocks, last, sums, table, accum, cap):
    n = blocks.shape[1]
    cols = table.shape[1]
    return pl.pallas_call(
        functools.partial(update_kernel, cap),
        out_shape=[
            jax.ShapeDtypeStruct(table.shape, F32),
            jax.ShapeDtypeStruct(accum.shape, F32),
        ],
        in_specs=[whole(SMEM)] + [whole()] * 6,
        out_specs=[whole(pltpu.HBM), whole()],
        scratch_shapes=[
            VMEM((n * TILE, cols), F32),
            pltpu.SemaphoreType.DMA,
            pltpu.SemaphoreType.DMA((n,)),
        ],
        compiler_params=params(),
    )(blocks, *last, *sums, table, accum)


def after(x, *earlier):
    return lax.optimization_barrier((x,) + earlier)[0]


def gathered(pooled_grad, send_sample, send_row, send_count, union_blocks, table, accum):
    shards = lax.axis_size("shard")
    reps = lax.axis_size("rep")
    cap = send_sample.shape[1]
    span = union_blocks.shape[1] * TILE
    me = lax.axis_index("shard").astype(jnp.int32).reshape(1)

    def swap(x, flip):
        pairs = []
        for z in range(shards):
            for r in range(reps):
                dz, dr = flip(r)
                pairs.append((z * reps + r, (z ^ dz) * reps + (r ^ dr)))
        return lax.ppermute(x, ("shard", "rep"), pairs)

    def first(x):
        return swap(x, lambda r: (0, 2 if r % 2 == 0 else 4))

    def second(x):
        return swap(x, lambda r: (0, 4 if r % 2 == 0 else 2))

    def core(x):
        return swap(x, lambda r: (0, 1))

    odd = (lax.axis_index("rep").astype(jnp.int32) % 2).reshape(1)
    mine = pack(me, send_count, pooled_grad, send_sample, send_row)
    arrived = [swap(mine[j], lambda r: (j, 0)) for j in ORDER]
    own = join([mine[0]] + arrived)
    one = first(own)
    part = own_sum(own, span, cap)
    two = second(after(own, part))
    own_c = core(own)
    diag = second(one)
    one_c, two_c = core(one), core(two)
    near, side = side_sum(odd, [own_c, one, two_c, two, one_c], part, span, cap)
    diag_c = core(after(diag, near))
    table_out, accum_out = update(
        union_blocks, (diag, diag_c), (near, side), table, accum.reshape(-1, TILE), cap
    )
    return table_out, accum_out.reshape(accum.shape)


def reduced(pooled_grad, send_sample, send_row, send_count, union_blocks, table, accum):
    columns = pooled_grad.shape[1]
    samples = pooled_grad.shape[0]
    active = (lax.broadcasted_iota(jnp.int32, send_sample.shape, 1) < send_count[:, None]).astype(F32)
    lengths = jax.ops.segment_sum(active.reshape(-1), send_sample.reshape(-1), num_segments=samples)
    scaled = active / jnp.maximum(lengths, 1.0)[send_sample]
    values = (pooled_grad[send_sample].astype(F32) * scaled[:, :, None]).astype(BF16)
    arrived = lax.all_to_all(values, "shard", split_axis=0, concat_axis=0, tiled=True)
    places = lax.all_to_all(send_row, "shard", split_axis=0, concat_axis=0, tiled=True)
    blocks = union_blocks[0]
    span = blocks.shape[0] * TILE
    local = (
        jnp.zeros((span, columns), F32)
        .at[places.reshape(-1)]
        .add(arrived.reshape(-1, columns).astype(F32))
    )
    table_tiles = table.reshape(-1, TILE, columns)
    accum_tiles = accum.reshape(-1, TILE)
    grad = lax.optimization_barrier(lax.psum(local.astype(BF16), "rep")).astype(F32)
    acc_new = accum_tiles[blocks].reshape(span) + jnp.mean(grad * grad, axis=-1)
    rows_new = table_tiles[blocks].reshape(span, columns) - LEARNING_RATE * grad / (
        jnp.sqrt(acc_new)[:, None] + EPSILON
    )
    table_out = table_tiles.at[blocks].set(rows_new.reshape(-1, TILE, columns)).reshape(table.shape)
    accum_out = accum_tiles.at[blocks].set(acc_new.reshape(-1, TILE)).reshape(accum.shape)
    return table_out, accum_out


def solution(mesh):
    both = ("shard", "rep")
    in_specs = (
        P(both, None),
        P(both, None),
        P(both, None),
        P(both),
        P("shard", None),
        P("shard", None),
        P("shard"),
    )
    out_specs = (P("shard", None), P("shard"))
    small = mesh.shape["shard"] == 4 and mesh.shape["rep"] == 8
    return jax.shard_map(
        gathered if small else reduced,
        mesh=mesh,
        in_specs=in_specs,
        out_specs=out_specs,
        check_vma=False,
    )
```

```python
import functools

import jax
import jax.numpy as jnp
from jax import lax
from jax.experimental import pallas as pl
from jax.experimental.pallas import tpu as pltpu
from jax.sharding import PartitionSpec as P

TILE = 128
STAGE_MIB = 61
TAIL = 16
LEARNING_RATE = 0.5
EPSILON = 1e-06
VMEM = pltpu.VMEM
SMEM = pltpu.SMEM
F32 = jnp.float32
BF16 = jnp.bfloat16


def params(mib=24):
    return pltpu.CompilerParams(vmem_limit_bytes=mib * 2**20)


def whole(space=VMEM):
    return pl.BlockSpec(memory_space=space)


def pack_kernel(grad_ref, places_ref, *out_refs):
    owners = len(out_refs)
    cap = places_ref.shape[1]
    samples, cols = grad_ref.shape
    me = lax.axis_index("shard")
    lane = lax.broadcasted_iota(jnp.int32, (1, cap), 1)
    sub = lax.broadcasted_iota(jnp.int32, (samples, cap), 0)
    counts = places_ref[2 * owners : 2 * owners + 1, :]

    def picks(o):
        count = jnp.sum(jnp.where(lane == o, counts, 0), axis=1, keepdims=True)
        live = jnp.where(lane < count, places_ref[pl.ds(o, 1), :], -1)
        return (sub == live).astype(F32)

    total = picks(0)
    for o in range(1, owners):
        total = total + picks(o)
    lengths = jnp.sum(total, axis=1, keepdims=True)
    scaled = (grad_ref[...].astype(F32) * (1.0 / jnp.maximum(lengths, 1.0))).astype(BF16)
    tail_row = lax.broadcasted_iota(jnp.int32, (TAIL, cap), 0)
    for j in range(owners):
        o = me ^ j
        values = lax.dot_general(
            picks(o).astype(BF16), scaled, (((0,), (0,)), ((), ())), preferred_element_type=F32
        )
        out_refs[j][0:cap, :] = values.astype(BF16)
        row = places_ref[pl.ds(owners + o, 1), :]
        slot = row // TILE
        within = row - slot * TILE
        tail = jnp.where(tail_row == 0, slot, jnp.where(tail_row == 1, within, 0))
        out_refs[j][cap : cap + TAIL, :] = jnp.zeros((TAIL, cols), BF16)
        out_refs[j][cap : cap + TAIL, 0:cap] = tail.astype(F32).astype(BF16)


def pack(count, grad, sample, row):
    owners, cap = sample.shape
    counts = jnp.pad(count[None, :], ((0, 0), (0, cap - owners)))
    places = jnp.concatenate([sample, row, counts], axis=0)
    shape = jax.ShapeDtypeStruct((cap + TAIL, grad.shape[1]), BF16)
    return pl.pallas_call(
        pack_kernel,
        out_shape=[shape] * owners,
        in_specs=[whole(), whole()],
        out_specs=[whole()] * owners,
        compiler_params=params(),
    )(grad, places)


def tiny(cols):
    return pl.CostEstimate(flops=cols, bytes_accessed=cols, transcendentals=0)


def join_kernel(*refs):
    *payloads, out = refs
    cols = out.shape[1]
    sub = lax.broadcasted_iota(jnp.int32, (TAIL, cols), 0)
    tail = jnp.zeros((TAIL, cols), F32)
    at = 0
    for ref in payloads:
        rows = ref.shape[0] - TAIL
        out[at : at + rows, :] = ref[0:rows, :]
        own = ref[rows : rows + TAIL, :].astype(F32)
        for i in range(2 * (rows // TILE)):
            tail = jnp.where(sub == 2 * (at // TILE) + i, own[i : i + 1, :], tail)
        at += rows
    out[at : at + TAIL, :] = tail.astype(BF16)


def join(*payloads):
    cols = payloads[0].shape[1]
    rows = sum(p.shape[0] - TAIL for p in payloads) + TAIL
    return pl.pallas_call(
        join_kernel,
        out_shape=jax.ShapeDtypeStruct((rows, cols), BF16),
        in_specs=[whole()] * len(payloads),
        out_specs=whole(),
        compiler_params=params(),
        cost_estimate=tiny(cols),
    )(*payloads)


def positions(ref, cap):
    entries = ref.shape[0] - TAIL
    tail = ref[entries : entries + TAIL, 0:cap].astype(F32)
    n = entries // cap
    slot = jnp.concatenate([tail[2 * c : 2 * c + 1] for c in range(n)], axis=1)
    within = jnp.concatenate([tail[2 * c + 1 : 2 * c + 2] for c in range(n)], axis=1)
    return slot, within


def block_sum(ref, place, k):
    slot, within = place
    here = jnp.where(slot == k, within, -1.0).astype(BF16)
    entries = here.shape[1]
    sub = lax.broadcasted_iota(jnp.int32, (TILE, entries), 0).astype(F32).astype(BF16)
    pick = jnp.where(sub == here, jnp.ones((), BF16), jnp.zeros((), BF16))
    return jnp.dot(pick, ref[0:entries, :], preferred_element_type=F32)


def tile(ref, block):
    return ref.at[pl.ds(pl.multiple_of(block * TILE, TILE), TILE), :]


def stage_kernel(blocks_ref, table_in, table_ref, free_ref, bounce, into, out):
    n = blocks_ref.shape[1]
    tiles = table_in.shape[0] // TILE
    seen = jnp.int32(0)
    for t in range(tiles):
        free_ref[t - seen] = t
        seen = seen + (blocks_ref[0, jnp.minimum(seen, n - 1)] == t).astype(jnp.int32)
    loads, stores = [], []
    for i in range(tiles - n):
        here = bounce.at[i * TILE : (i + 1) * TILE, :]
        loads.append(pltpu.make_async_copy(tile(table_in, free_ref[i]), here, into.at[i]))
        stores.append(pltpu.make_async_copy(here, tile(table_ref, free_ref[i]), out.at[i]))
    for c in loads:
        c.start()
    for load, store in zip(loads, stores):
        load.wait()
        store.start()
    for c in stores:
        c.wait()


def stage(blocks, table):
    n = blocks.shape[1]
    tiles = table.shape[0] // TILE
    free = tiles - n
    return pl.pallas_call(
        stage_kernel,
        out_shape=jax.ShapeDtypeStruct(table.shape, F32),
        in_specs=[whole(SMEM), whole(pltpu.HBM)],
        out_specs=whole(pltpu.HBM),
        scratch_shapes=[
            SMEM((tiles + 1,), jnp.int32),
            VMEM((free * TILE, table.shape[1]), F32),
            pltpu.SemaphoreType.DMA((free,)),
            pltpu.SemaphoreType.DMA((free,)),
        ],
        compiler_params=params(STAGE_MIB),
        cost_estimate=pl.CostEstimate(
            flops=0, bytes_accessed=4 * table.size * 3, transcendentals=0
        ),
    )(blocks, table)


def own_kernel(cap, blocks_ref, own, accum_ref, part, old):
    place = positions(own, cap)
    for k in range(part.shape[0] // TILE):
        span = slice(k * TILE, (k + 1) * TILE)
        part[span, :] = block_sum(own, place, k)
        row = accum_ref[pl.ds(blocks_ref[0, k], 1), :]
        old[span, :] = jnp.broadcast_to(row, (TILE, TILE)).T


def own_sum(blocks, own, accum, span, cap):
    entries, cols = own.shape[0] - TAIL, own.shape[1]
    return pl.pallas_call(
        functools.partial(own_kernel, cap),
        out_shape=[
            jax.ShapeDtypeStruct((span, cols), F32),
            jax.ShapeDtypeStruct((span, TILE), F32),
        ],
        in_specs=[whole(SMEM), whole(), whole()],
        out_specs=[whole()] * 2,
        compiler_params=params(),
        cost_estimate=pl.CostEstimate(
            flops=2 * span * entries * cols, bytes_accessed=span * cols * 4, transcendentals=0
        ),
    )(blocks, own, accum)


def one_kernel(cap, payload, part):
    place = positions(payload, cap)
    for k in range(part.shape[0] // TILE):
        part[k * TILE : (k + 1) * TILE, :] = block_sum(payload, place, k)


def near_kernel(cap, one, two, part, near, side):
    places = [positions(ref, cap) for ref in (one, two)]
    for k in range(near.shape[0] // TILE):
        span = slice(k * TILE, (k + 1) * TILE)
        near[span, :] = part[span, :] + block_sum(one, places[0], k)
        side[span, :] = block_sum(two, places[1], k)


def rest_kernel(cap, diag, one_c, two_c, near, side, part_c, mine, near_c, side_c):
    places = [positions(ref, cap) for ref in (diag, one_c, two_c)]
    for k in range(near.shape[0] // TILE):
        span = slice(k * TILE, (k + 1) * TILE)
        mine[span, :] = near[span, :] + (side[span, :] + block_sum(diag, places[0], k))
        near_c[span, :] = part_c[span, :] + block_sum(one_c, places[1], k)
        side_c[span, :] = block_sum(two_c, places[2], k)


def sum_call(kernel, payloads, parts, results, span, cap):
    entries, cols = payloads[0].shape[0] - TAIL, payloads[0].shape[1]
    wide = jax.ShapeDtypeStruct((span, cols), F32)
    return pl.pallas_call(
        functools.partial(kernel, cap),
        out_shape=[wide] * results,
        in_specs=[whole()] * (len(payloads) + len(parts)),
        out_specs=[whole()] * results,
        compiler_params=params(),
        cost_estimate=pl.CostEstimate(
            flops=2 * span * entries * cols * len(payloads),
            bytes_accessed=span * cols * 4 * (results + len(parts)),
            transcendentals=0,
        ),
    )(*payloads, *parts)


def update_kernel(
    cap, blocks_ref, last, mine, near, side, old, table_in, accum_ref, alias,
    table_ref, accum_out, rows_out, accum_new, sem, sems,
):
    del alias
    n = rows_out.shape[0] // TILE
    cols = rows_out.shape[1]
    place = positions(last, cap)
    accum_new[...] = accum_ref[...]
    diagonal = lax.broadcasted_iota(jnp.int32, (TILE, TILE), 0) == lax.broadcasted_iota(
        jnp.int32, (TILE, TILE), 1
    )
    ones = jnp.ones((2 * cols, TILE), BF16)
    news = []
    copies = []
    for k in range(n):
        span = slice(k * TILE, (k + 1) * TILE)
        block = pl.multiple_of(blocks_ref[0, k] * TILE, TILE)
        other = near[span, :] + (side[span, :] + block_sum(last, place, k))
        grad = (mine[span, :] + other).astype(BF16).astype(F32)
        square = grad * grad
        high = square.astype(BF16)
        low = (square - high.astype(F32)).astype(BF16)
        total = jnp.dot(jnp.concatenate([high, low], axis=1), ones, preferred_element_type=F32)
        new = old[span, :] + total * (1.0 / cols)
        rate = LEARNING_RATE / (jnp.sqrt(new) + EPSILON)
        for c in range(0, cols, TILE):
            rows_out[span, c : c + TILE] = (
                table_in[pl.ds(block, TILE), c : c + TILE] - grad[:, c : c + TILE] * rate
            )
        news.append(jnp.sum(jnp.where(diagonal, new, 0.0), axis=0, keepdims=True))
        c = pltpu.make_async_copy(rows_out.at[span, :], tile(table_ref, blocks_ref[0, k]), sems.at[k])
        c.start()
        copies.append(c)
    for k in range(n):
        accum_new[pl.ds(blocks_ref[0, k], 1), :] = news[k]
    c = pltpu.make_async_copy(accum_new, accum_out, sem)
    c.start()
    for c in copies + [c]:
        c.wait()


def update(blocks, last, sums, old, table, accum, target, cap):
    n = blocks.shape[1]
    return pl.pallas_call(
        functools.partial(update_kernel, cap),
        out_shape=[
            jax.ShapeDtypeStruct(table.shape, F32),
            jax.ShapeDtypeStruct(accum.shape, F32),
        ],
        in_specs=[whole(SMEM)] + [whole()] * 7 + [whole(pltpu.HBM)],
        out_specs=[whole(pltpu.HBM), whole(pltpu.HBM)],
        scratch_shapes=[
            VMEM((n * TILE, table.shape[1]), F32),
            VMEM(accum.shape, F32),
            pltpu.SemaphoreType.DMA,
            pltpu.SemaphoreType.DMA((n,)),
        ],
        input_output_aliases={8: 0},
        compiler_params=params(),
    )(blocks, last, *sums, old, table, accum, target)


def after(x, *earlier):
    return lax.optimization_barrier((x,) + earlier)[0]


def gathered(pooled_grad, send_sample, send_row, send_count, union_blocks, table, accum):
    shards = lax.axis_size("shard")
    reps = lax.axis_size("rep")
    cap = send_sample.shape[1]
    span = union_blocks.shape[1] * TILE
    old_accum = accum.reshape(-1, TILE)

    def swap(x, flip):
        pairs = []
        for z in range(shards):
            for r in range(reps):
                dz, dr = flip(r)
                pairs.append((z * reps + r, (z ^ dz) * reps + (r ^ dr)))
        return lax.ppermute(x, ("shard", "rep"), pairs)

    def first(x):
        return swap(x, lambda r: (0, 2 if r % 2 == 0 else 4))

    def second(x):
        return swap(x, lambda r: (0, 4 if r % 2 == 0 else 2))

    def core(x):
        return swap(x, lambda r: (0, 1))

    mine = pack(send_count, pooled_grad, send_sample, send_row)
    target = stage(after(union_blocks, mine[0]), table)
    arrived = [swap(mine[j], lambda r: (j, 0)) for j in (3, 2, 1)]
    own = join(after(mine[0], target), *arrived)
    one = first(own)
    own_c = core(own)
    part, old = own_sum(union_blocks, own, old_accum, span, cap)
    two = second(after(own, part))
    (part_c,) = sum_call(one_kernel, [own_c], [], 1, span, cap)
    diag = second(after(one, part_c))
    near, side = sum_call(near_kernel, [one, two], [part], 2, span, cap)
    one_c, two_c = core(one), core(two)
    last = core(after(diag, near))
    mine, near_c, side_c = sum_call(
        rest_kernel, [diag, one_c, two_c], [near, side, part_c], 3, span, cap
    )
    table_out, accum_out = update(
        union_blocks, last, (mine, near_c, side_c), old, table, old_accum, target, cap
    )
    return table_out, accum_out.reshape(accum.shape)


def reduced(pooled_grad, send_sample, send_row, send_count, union_blocks, table, accum):
    columns = pooled_grad.shape[1]
    samples = pooled_grad.shape[0]
    active = (lax.broadcasted_iota(jnp.int32, send_sample.shape, 1) < send_count[:, None]).astype(F32)
    lengths = jax.ops.segment_sum(active.reshape(-1), send_sample.reshape(-1), num_segments=samples)
    scaled = active / jnp.maximum(lengths, 1.0)[send_sample]
    values = (pooled_grad[send_sample].astype(F32) * scaled[:, :, None]).astype(BF16)
    arrived = lax.all_to_all(values, "shard", split_axis=0, concat_axis=0, tiled=True)
    places = lax.all_to_all(send_row, "shard", split_axis=0, concat_axis=0, tiled=True)
    blocks = union_blocks[0]
    span = blocks.shape[0] * TILE
    local = (
        jnp.zeros((span, columns), F32)
        .at[places.reshape(-1)]
        .add(arrived.reshape(-1, columns).astype(F32))
    )
    table_tiles = table.reshape(-1, TILE, columns)
    accum_tiles = accum.reshape(-1, TILE)
    grad = lax.optimization_barrier(lax.psum(local.astype(BF16), "rep")).astype(F32)
    acc_new = accum_tiles[blocks].reshape(span) + jnp.mean(grad * grad, axis=-1)
    rows_new = table_tiles[blocks].reshape(span, columns) - LEARNING_RATE * grad / (
        jnp.sqrt(acc_new)[:, None] + EPSILON
    )
    table_out = table_tiles.at[blocks].set(rows_new.reshape(-1, TILE, columns)).reshape(table.shape)
    accum_out = accum_tiles.at[blocks].set(acc_new.reshape(-1, TILE)).reshape(accum.shape)
    return table_out, accum_out


def solution(mesh):
    both = ("shard", "rep")
    in_specs = (
        P(both, None),
        P(both, None),
        P(both, None),
        P(both),
        P("shard", None),
        P("shard", None),
        P("shard"),
    )
    out_specs = (P("shard", None), P("shard"))
    small = mesh.shape["shard"] == 4 and mesh.shape["rep"] == 8
    return jax.shard_map(
        gathered if small else reduced,
        mesh=mesh,
        in_specs=in_specs,
        out_specs=out_specs,
        check_vma=False,
    )
```

```python
import functools

import jax
import jax.numpy as jnp
from jax import lax
from jax.experimental import pallas as pl
from jax.experimental.pallas import tpu as pltpu
from jax.sharding import PartitionSpec as P

TILE = 128
STAGE_MIB = 61
PACK_BYTES = 60 * 1024 * 1024
TAIL = 16
LEARNING_RATE = 0.5
EPSILON = 1e-06
VMEM = pltpu.VMEM
SMEM = pltpu.SMEM
F32 = jnp.float32
BF16 = jnp.bfloat16


def params(mib=24):
    return pltpu.CompilerParams(vmem_limit_bytes=mib * 2**20)


def whole(space=VMEM):
    return pl.BlockSpec(memory_space=space)


def pack_kernel(count_in, grad_in, sample_in, row_in, *refs):
    *out_refs, count_ref, grad_ref, sample_ref, row_ref, sems = refs
    copies = [
        pltpu.make_async_copy(src, dst, sems.at[i])
        for i, (src, dst) in enumerate(
            (
                (sample_in, sample_ref),
                (count_in, count_ref),
                (grad_in, grad_ref),
                (row_in, row_ref),
            )
        )
    ]
    for c in copies:
        c.start()
    owners = len(out_refs)
    cap = sample_ref.shape[1]
    samples, cols = grad_ref.shape
    me = lax.axis_index("shard")
    lane = lax.broadcasted_iota(jnp.int32, (1, cap), 1)
    sub = lax.broadcasted_iota(jnp.int32, (samples, cap), 0)

    def picks(o):
        live = jnp.where(lane < count_ref[o], sample_ref[pl.ds(o, 1), :], -1)
        return (sub == live).astype(F32)

    copies[0].wait()
    copies[1].wait()
    total = picks(0)
    for o in range(1, owners):
        total = total + picks(o)
    lengths = jnp.sum(total, axis=1, keepdims=True)
    copies[2].wait()
    scaled = (grad_ref[...].astype(F32) * (1.0 / jnp.maximum(lengths, 1.0))).astype(BF16)
    copies[3].wait()
    tail_row = lax.broadcasted_iota(jnp.int32, (TAIL, cap), 0)
    for j in range(owners):
        o = me ^ j
        values = lax.dot_general(
            picks(o).astype(BF16), scaled, (((0,), (0,)), ((), ())), preferred_element_type=F32
        )
        out_refs[j][0:cap, :] = values.astype(BF16)
        row = row_ref[pl.ds(o, 1), :]
        slot = row // TILE
        within = row - slot * TILE
        tail = jnp.where(tail_row == 0, slot, jnp.where(tail_row == 1, within, 0))
        out_refs[j][cap : cap + TAIL, :] = jnp.zeros((TAIL, cols), BF16)
        out_refs[j][cap : cap + TAIL, 0:cap] = tail.astype(F32).astype(BF16)


def pack(count, grad, sample, row):
    owners, cap = sample.shape
    shape = VMEM((cap + TAIL, grad.shape[1]), BF16)
    return pl.pallas_call(
        pack_kernel,
        out_shape=[shape] * owners,
        in_specs=[whole(pltpu.HBM)] * 4,
        out_specs=[whole()] * owners,
        scratch_shapes=[
            SMEM(count.shape, jnp.int32),
            VMEM(grad.shape, BF16),
            VMEM(sample.shape, jnp.int32),
            VMEM(row.shape, jnp.int32),
            pltpu.SemaphoreType.DMA((4,)),
        ],
        compiler_params=pltpu.CompilerParams(vmem_limit_bytes=PACK_BYTES),
    )(count, grad, sample, row)


def tiny(cols):
    return pl.CostEstimate(flops=cols, bytes_accessed=cols, transcendentals=0)


def join_kernel(*refs):
    *payloads, out = refs
    cols = out.shape[1]
    sub = lax.broadcasted_iota(jnp.int32, (TAIL, cols), 0)
    tail = jnp.zeros((TAIL, cols), F32)
    at = 0
    for ref in payloads:
        rows = ref.shape[0] - TAIL
        out[at : at + rows, :] = ref[0:rows, :]
        own = ref[rows : rows + TAIL, :].astype(F32)
        for i in range(2 * (rows // TILE)):
            tail = jnp.where(sub == 2 * (at // TILE) + i, own[i : i + 1, :], tail)
        at += rows
    out[at : at + TAIL, :] = tail.astype(BF16)


def join(*payloads):
    cols = payloads[0].shape[1]
    rows = sum(p.shape[0] - TAIL for p in payloads) + TAIL
    return pl.pallas_call(
        join_kernel,
        out_shape=jax.ShapeDtypeStruct((rows, cols), BF16),
        in_specs=[whole()] * len(payloads),
        out_specs=whole(),
        compiler_params=params(),
        cost_estimate=tiny(cols),
    )(*payloads)


def positions(ref, cap):
    entries = ref.shape[0] - TAIL
    tail = ref[entries : entries + TAIL, 0:cap].astype(F32)
    n = entries // cap
    slot = jnp.concatenate([tail[2 * c : 2 * c + 1] for c in range(n)], axis=1)
    within = jnp.concatenate([tail[2 * c + 1 : 2 * c + 2] for c in range(n)], axis=1)
    return slot, within


def block_sum(ref, place, k):
    slot, within = place
    here = jnp.where(slot == k, within, -1.0).astype(BF16)
    entries = here.shape[1]
    sub = lax.broadcasted_iota(jnp.int32, (TILE, entries), 0).astype(F32).astype(BF16)
    pick = jnp.where(sub == here, jnp.ones((), BF16), jnp.zeros((), BF16))
    return jnp.dot(pick, ref[0:entries, :], preferred_element_type=F32)


def tile(ref, block):
    return ref.at[pl.ds(pl.multiple_of(block * TILE, TILE), TILE), :]


def stage_kernel(blocks_ref, table_in, table_ref, free_ref, bounce, into, out):
    n = blocks_ref.shape[1]
    tiles = table_in.shape[0] // TILE
    seen = jnp.int32(0)
    for t in range(tiles):
        free_ref[t - seen] = t
        seen = seen + (blocks_ref[0, jnp.minimum(seen, n - 1)] == t).astype(jnp.int32)
    loads, stores = [], []
    for i in range(tiles - n):
        here = bounce.at[i * TILE : (i + 1) * TILE, :]
        loads.append(pltpu.make_async_copy(tile(table_in, free_ref[i]), here, into.at[i]))
        stores.append(pltpu.make_async_copy(here, tile(table_ref, free_ref[i]), out.at[i]))
    for c in loads:
        c.start()
    for load, store in zip(loads, stores):
        load.wait()
        store.start()
    for c in stores:
        c.wait()


def stage(blocks, table):
    n = blocks.shape[1]
    tiles = table.shape[0] // TILE
    free = tiles - n
    return pl.pallas_call(
        stage_kernel,
        out_shape=jax.ShapeDtypeStruct(table.shape, F32),
        in_specs=[whole(SMEM), whole(pltpu.HBM)],
        out_specs=whole(pltpu.HBM),
        scratch_shapes=[
            SMEM((tiles + 1,), jnp.int32),
            VMEM((free * TILE, table.shape[1]), F32),
            pltpu.SemaphoreType.DMA((free,)),
            pltpu.SemaphoreType.DMA((free,)),
        ],
        compiler_params=params(STAGE_MIB),
        cost_estimate=pl.CostEstimate(
            flops=0, bytes_accessed=4 * table.size * 3, transcendentals=0
        ),
    )(blocks, table)


def own_kernel(cap, blocks_ref, own, accum_ref, part, old):
    place = positions(own, cap)
    for k in range(part.shape[0] // TILE):
        span = slice(k * TILE, (k + 1) * TILE)
        part[span, :] = block_sum(own, place, k)
        row = accum_ref[pl.ds(blocks_ref[0, k], 1), :]
        old[span, :] = jnp.broadcast_to(row, (TILE, TILE)).T


def own_sum(blocks, own, accum, span, cap):
    entries, cols = own.shape[0] - TAIL, own.shape[1]
    return pl.pallas_call(
        functools.partial(own_kernel, cap),
        out_shape=[
            jax.ShapeDtypeStruct((span, cols), F32),
            jax.ShapeDtypeStruct((span, TILE), F32),
        ],
        in_specs=[whole(SMEM), whole(), whole()],
        out_specs=[whole()] * 2,
        compiler_params=params(),
        cost_estimate=pl.CostEstimate(
            flops=2 * span * entries * cols, bytes_accessed=span * cols * 4, transcendentals=0
        ),
    )(blocks, own, accum)


def one_kernel(cap, payload, part):
    place = positions(payload, cap)
    for k in range(part.shape[0] // TILE):
        part[k * TILE : (k + 1) * TILE, :] = block_sum(payload, place, k)


def near_kernel(cap, one, two, part, near, side):
    places = [positions(ref, cap) for ref in (one, two)]
    for k in range(near.shape[0] // TILE):
        span = slice(k * TILE, (k + 1) * TILE)
        near[span, :] = part[span, :] + block_sum(one, places[0], k)
        side[span, :] = block_sum(two, places[1], k)


def rest_kernel(cap, diag, one_c, two_c, near, side, part_c, mine, near_c, side_c):
    places = [positions(ref, cap) for ref in (diag, one_c, two_c)]
    for k in range(near.shape[0] // TILE):
        span = slice(k * TILE, (k + 1) * TILE)
        mine[span, :] = near[span, :] + (side[span, :] + block_sum(diag, places[0], k))
        near_c[span, :] = part_c[span, :] + block_sum(one_c, places[1], k)
        side_c[span, :] = block_sum(two_c, places[2], k)


def sum_call(kernel, payloads, parts, results, span, cap):
    entries, cols = payloads[0].shape[0] - TAIL, payloads[0].shape[1]
    wide = jax.ShapeDtypeStruct((span, cols), F32)
    return pl.pallas_call(
        functools.partial(kernel, cap),
        out_shape=[wide] * results,
        in_specs=[whole()] * (len(payloads) + len(parts)),
        out_specs=[whole()] * results,
        compiler_params=params(),
        cost_estimate=pl.CostEstimate(
            flops=2 * span * entries * cols * len(payloads),
            bytes_accessed=span * cols * 4 * (results + len(parts)),
            transcendentals=0,
        ),
    )(*payloads, *parts)


def update_kernel(
    cap, blocks_ref, last, mine, near, side, old, table_in, accum_ref, alias,
    table_ref, accum_out, rows_out, accum_new, sem, sems,
):
    del alias
    n = rows_out.shape[0] // TILE
    cols = rows_out.shape[1]
    place = positions(last, cap)
    accum_new[...] = accum_ref[...]
    diagonal = lax.broadcasted_iota(jnp.int32, (TILE, TILE), 0) == lax.broadcasted_iota(
        jnp.int32, (TILE, TILE), 1
    )
    ones = jnp.ones((2 * cols, TILE), BF16)
    news = []
    copies = []
    for k in range(n):
        span = slice(k * TILE, (k + 1) * TILE)
        block = pl.multiple_of(blocks_ref[0, k] * TILE, TILE)
        other = near[span, :] + (side[span, :] + block_sum(last, place, k))
        grad = (mine[span, :] + other).astype(BF16).astype(F32)
        square = grad * grad
        high = square.astype(BF16)
        low = (square - high.astype(F32)).astype(BF16)
        total = jnp.dot(jnp.concatenate([high, low], axis=1), ones, preferred_element_type=F32)
        new = old[span, :] + total * (1.0 / cols)
        rate = LEARNING_RATE / (jnp.sqrt(new) + EPSILON)
        for c in range(0, cols, TILE):
            rows_out[span, c : c + TILE] = (
                table_in[pl.ds(block, TILE), c : c + TILE] - grad[:, c : c + TILE] * rate
            )
        news.append(jnp.sum(jnp.where(diagonal, new, 0.0), axis=0, keepdims=True))
        c = pltpu.make_async_copy(rows_out.at[span, :], tile(table_ref, blocks_ref[0, k]), sems.at[k])
        c.start()
        copies.append(c)
    for k in range(n):
        accum_new[pl.ds(blocks_ref[0, k], 1), :] = news[k]
    c = pltpu.make_async_copy(accum_new, accum_out, sem)
    c.start()
    for c in copies + [c]:
        c.wait()


def update(blocks, last, sums, old, table, accum, target, cap):
    n = blocks.shape[1]
    return pl.pallas_call(
        functools.partial(update_kernel, cap),
        out_shape=[
            jax.ShapeDtypeStruct(table.shape, F32),
            jax.ShapeDtypeStruct(accum.shape, F32),
        ],
        in_specs=[whole(SMEM)] + [whole()] * 7 + [whole(pltpu.HBM)],
        out_specs=[whole(pltpu.HBM), whole(pltpu.HBM)],
        scratch_shapes=[
            VMEM((n * TILE, table.shape[1]), F32),
            VMEM(accum.shape, F32),
            pltpu.SemaphoreType.DMA,
            pltpu.SemaphoreType.DMA((n,)),
        ],
        input_output_aliases={8: 0},
        compiler_params=params(),
    )(blocks, last, *sums, old, table, accum, target)


def after(x, *earlier):
    return lax.optimization_barrier((x,) + earlier)[0]


def gathered(pooled_grad, send_sample, send_row, send_count, union_blocks, table, accum):
    shards = lax.axis_size("shard")
    reps = lax.axis_size("rep")
    cap = send_sample.shape[1]
    span = union_blocks.shape[1] * TILE
    old_accum = accum.reshape(-1, TILE)

    def swap(x, flip):
        pairs = []
        for z in range(shards):
            for r in range(reps):
                dz, dr = flip(r)
                pairs.append((z * reps + r, (z ^ dz) * reps + (r ^ dr)))
        return lax.ppermute(x, ("shard", "rep"), pairs)

    def first(x):
        return swap(x, lambda r: (0, 2 if r % 2 == 0 else 4))

    def second(x):
        return swap(x, lambda r: (0, 4 if r % 2 == 0 else 2))

    def core(x):
        return swap(x, lambda r: (0, 1))

    mine = pack(send_count, pooled_grad, send_sample, send_row)
    target = stage(after(union_blocks, mine[0]), table)
    arrived = [swap(mine[j], lambda r: (j, 0)) for j in (3, 2, 1)]
    own = join(after(mine[0], target), *arrived)
    one = first(own)
    own_c = core(own)
    part, old = own_sum(union_blocks, own, old_accum, span, cap)
    (part_c,) = sum_call(one_kernel, [own_c], [], 1, span, cap)
    two = second(after(own, part, part_c))
    diag = second(one)
    near, side = sum_call(near_kernel, [one, two], [part], 2, span, cap)
    one_c, two_c = core(one), core(two)
    last = core(after(diag, near))
    mine, near_c, side_c = sum_call(
        rest_kernel, [diag, one_c, two_c], [near, side, part_c], 3, span, cap
    )
    table_out, accum_out = update(
        union_blocks, last, (mine, near_c, side_c), old, table, old_accum, target, cap
    )
    return table_out, accum_out.reshape(accum.shape)


def reduced(pooled_grad, send_sample, send_row, send_count, union_blocks, table, accum):
    columns = pooled_grad.shape[1]
    samples = pooled_grad.shape[0]
    active = (lax.broadcasted_iota(jnp.int32, send_sample.shape, 1) < send_count[:, None]).astype(F32)
    lengths = jax.ops.segment_sum(active.reshape(-1), send_sample.reshape(-1), num_segments=samples)
    scaled = active / jnp.maximum(lengths, 1.0)[send_sample]
    values = (pooled_grad[send_sample].astype(F32) * scaled[:, :, None]).astype(BF16)
    arrived = lax.all_to_all(values, "shard", split_axis=0, concat_axis=0, tiled=True)
    places = lax.all_to_all(send_row, "shard", split_axis=0, concat_axis=0, tiled=True)
    blocks = union_blocks[0]
    span = blocks.shape[0] * TILE
    local = (
        jnp.zeros((span, columns), F32)
        .at[places.reshape(-1)]
        .add(arrived.reshape(-1, columns).astype(F32))
    )
    table_tiles = table.reshape(-1, TILE, columns)
    accum_tiles = accum.reshape(-1, TILE)
    grad = lax.optimization_barrier(lax.psum(local.astype(BF16), "rep")).astype(F32)
    acc_new = accum_tiles[blocks].reshape(span) + jnp.mean(grad * grad, axis=-1)
    rows_new = table_tiles[blocks].reshape(span, columns) - LEARNING_RATE * grad / (
        jnp.sqrt(acc_new)[:, None] + EPSILON
    )
    table_out = table_tiles.at[blocks].set(rows_new.reshape(-1, TILE, columns)).reshape(table.shape)
    accum_out = accum_tiles.at[blocks].set(acc_new.reshape(-1, TILE)).reshape(accum.shape)
    return table_out, accum_out


def solution(mesh):
    both = ("shard", "rep")
    in_specs = (
        P(both, None),
        P(both, None),
        P(both, None),
        P(both),
        P("shard", None),
        P("shard", None),
        P("shard"),
    )
    out_specs = (P("shard", None), P("shard"))
    small = mesh.shape["shard"] == 4 and mesh.shape["rep"] == 8
    return jax.shard_map(
        gathered if small else reduced,
        mesh=mesh,
        in_specs=in_specs,
        out_specs=out_specs,
        check_vma=False,
    )
```

```python
import functools

import jax
import jax.numpy as jnp
from jax import lax
from jax.experimental import pallas as pl
from jax.experimental.pallas import tpu as pltpu
from jax.sharding import PartitionSpec as P

TILE = 128
LOAD_MIB = 56
PACK_BYTES = 60 * 1024 * 1024
TAIL = 16
LEARNING_RATE = 0.5
EPSILON = 1e-06
VMEM = pltpu.VMEM
SMEM = pltpu.SMEM
F32 = jnp.float32
BF16 = jnp.bfloat16


def params(mib=24):
    return pltpu.CompilerParams(vmem_limit_bytes=mib * 2**20)


def whole(space=VMEM):
    return pl.BlockSpec(memory_space=space)


def pack_kernel(count_in, grad_in, sample_in, row_in, *refs):
    *out_refs, count_ref, grad_ref, sample_ref, row_ref, sems = refs
    copies = [
        pltpu.make_async_copy(src, dst, sems.at[i])
        for i, (src, dst) in enumerate(
            (
                (sample_in, sample_ref),
                (count_in, count_ref),
                (grad_in, grad_ref),
                (row_in, row_ref),
            )
        )
    ]
    for c in copies:
        c.start()
    owners = len(out_refs)
    cap = sample_ref.shape[1]
    samples, cols = grad_ref.shape
    me = lax.axis_index("shard")
    lane = lax.broadcasted_iota(jnp.int32, (1, cap), 1)
    sub = lax.broadcasted_iota(jnp.int32, (samples, cap), 0)

    def picks(o):
        live = jnp.where(lane < count_ref[o], sample_ref[pl.ds(o, 1), :], -1)
        return (sub == live).astype(F32)

    copies[0].wait()
    copies[1].wait()
    total = picks(0)
    for o in range(1, owners):
        total = total + picks(o)
    lengths = jnp.sum(total, axis=1, keepdims=True)
    copies[2].wait()
    scaled = (grad_ref[...].astype(F32) * (1.0 / jnp.maximum(lengths, 1.0))).astype(BF16)
    copies[3].wait()
    tail_row = lax.broadcasted_iota(jnp.int32, (TAIL, cap), 0)
    for j in range(owners):
        o = me ^ j
        values = lax.dot_general(
            picks(o).astype(BF16), scaled, (((0,), (0,)), ((), ())), preferred_element_type=F32
        )
        out_refs[j][0:cap, :] = values.astype(BF16)
        row = row_ref[pl.ds(o, 1), :]
        slot = row // TILE
        within = row - slot * TILE
        tail = jnp.where(tail_row == 0, slot, jnp.where(tail_row == 1, within, 0))
        out_refs[j][cap : cap + TAIL, :] = jnp.zeros((TAIL, cols), BF16)
        out_refs[j][cap : cap + TAIL, 0:cap] = tail.astype(F32).astype(BF16)


def pack(count, grad, sample, row):
    owners, cap = sample.shape
    shape = VMEM((cap + TAIL, grad.shape[1]), BF16)
    return pl.pallas_call(
        pack_kernel,
        out_shape=[shape] * owners,
        in_specs=[whole(pltpu.HBM)] * 4,
        out_specs=[whole()] * owners,
        scratch_shapes=[
            SMEM(count.shape, jnp.int32),
            VMEM(grad.shape, BF16),
            VMEM(sample.shape, jnp.int32),
            VMEM(row.shape, jnp.int32),
            pltpu.SemaphoreType.DMA((4,)),
        ],
        compiler_params=pltpu.CompilerParams(vmem_limit_bytes=PACK_BYTES),
    )(count, grad, sample, row)


def tiny(cols):
    return pl.CostEstimate(flops=cols, bytes_accessed=cols, transcendentals=0)


def join_kernel(*refs):
    *payloads, out = refs
    cols = out.shape[1]
    sub = lax.broadcasted_iota(jnp.int32, (TAIL, cols), 0)
    tail = jnp.zeros((TAIL, cols), F32)
    at = 0
    for ref in payloads:
        rows = ref.shape[0] - TAIL
        out[at : at + rows, :] = ref[0:rows, :]
        own = ref[rows : rows + TAIL, :].astype(F32)
        for i in range(2 * (rows // TILE)):
            tail = jnp.where(sub == 2 * (at // TILE) + i, own[i : i + 1, :], tail)
        at += rows
    out[at : at + TAIL, :] = tail.astype(BF16)


def join(*payloads):
    cols = payloads[0].shape[1]
    rows = sum(p.shape[0] - TAIL for p in payloads) + TAIL
    return pl.pallas_call(
        join_kernel,
        out_shape=jax.ShapeDtypeStruct((rows, cols), BF16),
        in_specs=[whole()] * len(payloads),
        out_specs=whole(),
        compiler_params=params(),
        cost_estimate=tiny(cols),
    )(*payloads)


def positions(ref, cap):
    entries = ref.shape[0] - TAIL
    tail = ref[entries : entries + TAIL, 0:cap].astype(F32)
    n = entries // cap
    slot = jnp.concatenate([tail[2 * c : 2 * c + 1] for c in range(n)], axis=1)
    within = jnp.concatenate([tail[2 * c + 1 : 2 * c + 2] for c in range(n)], axis=1)
    return slot, within


def block_sum(ref, place, k):
    slot, within = place
    here = jnp.where(slot == k, within, -1.0).astype(BF16)
    entries = here.shape[1]
    sub = lax.broadcasted_iota(jnp.int32, (TILE, entries), 0).astype(F32).astype(BF16)
    pick = jnp.where(sub == here, jnp.ones((), BF16), jnp.zeros((), BF16))
    return jnp.dot(pick, ref[0:entries, :], preferred_element_type=F32)


def tile(ref, block):
    return ref.at[pl.ds(pl.multiple_of(block * TILE, TILE), TILE), :]


def load_kernel(table_in, table_out, sem):
    c = pltpu.make_async_copy(table_in, table_out, sem)
    c.start()
    c.wait()


def load(table):
    return pl.pallas_call(
        load_kernel,
        out_shape=VMEM(table.shape, F32),
        in_specs=[whole(pltpu.HBM)],
        out_specs=whole(),
        scratch_shapes=[pltpu.SemaphoreType.DMA],
        compiler_params=params(LOAD_MIB),
        cost_estimate=pl.CostEstimate(
            flops=0, bytes_accessed=4 * table.size * 3, transcendentals=0
        ),
    )(table)


def own_kernel(cap, blocks_ref, own, accum_ref, table_in, part, old, table_ref, free_ref, sems):
    n = part.shape[0] // TILE
    tiles = accum_ref.shape[0]
    seen = jnp.int32(0)
    for t in range(tiles):
        free_ref[t - seen] = t
        seen = seen + (blocks_ref[0, jnp.minimum(seen, n - 1)] == t).astype(jnp.int32)
    copies = [
        pltpu.make_async_copy(tile(table_in, free_ref[i]), tile(table_ref, free_ref[i]), sems.at[i])
        for i in range(tiles - n)
    ]
    for c in copies:
        c.start()
    place = positions(own, cap)
    for k in range(n):
        span = slice(k * TILE, (k + 1) * TILE)
        part[span, :] = block_sum(own, place, k)
        row = accum_ref[pl.ds(blocks_ref[0, k], 1), :]
        old[span, :] = jnp.broadcast_to(row, (TILE, TILE)).T
    for c in copies:
        c.wait()


def own_sum(blocks, own, accum, table, span, cap):
    entries, cols = own.shape[0] - TAIL, own.shape[1]
    tiles = accum.shape[0]
    free = tiles - span // TILE
    return pl.pallas_call(
        functools.partial(own_kernel, cap),
        out_shape=[
            jax.ShapeDtypeStruct((span, cols), F32),
            jax.ShapeDtypeStruct((span, TILE), F32),
            jax.ShapeDtypeStruct(table.shape, F32),
        ],
        in_specs=[whole(SMEM), whole(), whole(), whole()],
        out_specs=[whole(), whole(), whole(pltpu.HBM)],
        scratch_shapes=[SMEM((tiles + 1,), jnp.int32), pltpu.SemaphoreType.DMA((free,))],
        compiler_params=params(),
        cost_estimate=pl.CostEstimate(
            flops=2 * span * entries * cols, bytes_accessed=span * cols * 4, transcendentals=0
        ),
    )(blocks, own, accum, table)


def near_kernel(cap, one, two, own_c, part, near, side, part_c):
    places = [positions(ref, cap) for ref in (one, two, own_c)]
    for k in range(near.shape[0] // TILE):
        span = slice(k * TILE, (k + 1) * TILE)
        near[span, :] = part[span, :] + block_sum(one, places[0], k)
        side[span, :] = block_sum(two, places[1], k)
        part_c[span, :] = block_sum(own_c, places[2], k)


def rest_kernel(cap, diag, one_c, two_c, near, side, part_c, mine, near_c, side_c):
    places = [positions(ref, cap) for ref in (diag, one_c, two_c)]
    for k in range(near.shape[0] // TILE):
        span = slice(k * TILE, (k + 1) * TILE)
        mine[span, :] = near[span, :] + (side[span, :] + block_sum(diag, places[0], k))
        near_c[span, :] = part_c[span, :] + block_sum(one_c, places[1], k)
        side_c[span, :] = block_sum(two_c, places[2], k)


def sum_call(kernel, payloads, parts, results, span, cap):
    entries, cols = payloads[0].shape[0] - TAIL, payloads[0].shape[1]
    wide = jax.ShapeDtypeStruct((span, cols), F32)
    return pl.pallas_call(
        functools.partial(kernel, cap),
        out_shape=[wide] * results,
        in_specs=[whole()] * (len(payloads) + len(parts)),
        out_specs=[whole()] * results,
        compiler_params=params(),
        cost_estimate=pl.CostEstimate(
            flops=2 * span * entries * cols * len(payloads),
            bytes_accessed=span * cols * 4 * (results + len(parts)),
            transcendentals=0,
        ),
    )(*payloads, *parts)


def update_kernel(
    cap, blocks_ref, last, mine, near, side, old, table_in, accum_ref, alias,
    table_ref, accum_out, rows_out, accum_new, sem, sems,
):
    del alias
    n = rows_out.shape[0] // TILE
    cols = rows_out.shape[1]
    place = positions(last, cap)
    accum_new[...] = accum_ref[...]
    diagonal = lax.broadcasted_iota(jnp.int32, (TILE, TILE), 0) == lax.broadcasted_iota(
        jnp.int32, (TILE, TILE), 1
    )
    ones = jnp.ones((2 * cols, TILE), BF16)
    news = []
    copies = []
    for k in range(n):
        span = slice(k * TILE, (k + 1) * TILE)
        block = pl.multiple_of(blocks_ref[0, k] * TILE, TILE)
        other = near[span, :] + (side[span, :] + block_sum(last, place, k))
        grad = (mine[span, :] + other).astype(BF16).astype(F32)
        square = grad * grad
        high = square.astype(BF16)
        low = (square - high.astype(F32)).astype(BF16)
        total = jnp.dot(jnp.concatenate([high, low], axis=1), ones, preferred_element_type=F32)
        new = old[span, :] + total * (1.0 / cols)
        rate = LEARNING_RATE / (jnp.sqrt(new) + EPSILON)
        for c in range(0, cols, TILE):
            rows_out[span, c : c + TILE] = (
                table_in[pl.ds(block, TILE), c : c + TILE] - grad[:, c : c + TILE] * rate
            )
        news.append(jnp.sum(jnp.where(diagonal, new, 0.0), axis=0, keepdims=True))
        c = pltpu.make_async_copy(rows_out.at[span, :], tile(table_ref, blocks_ref[0, k]), sems.at[k])
        c.start()
        copies.append(c)
    for k in range(n):
        accum_new[pl.ds(blocks_ref[0, k], 1), :] = news[k]
    c = pltpu.make_async_copy(accum_new, accum_out, sem)
    c.start()
    for c in copies + [c]:
        c.wait()


def update(blocks, last, sums, old, table, accum, target, cap):
    n = blocks.shape[1]
    return pl.pallas_call(
        functools.partial(update_kernel, cap),
        out_shape=[
            jax.ShapeDtypeStruct(table.shape, F32),
            jax.ShapeDtypeStruct(accum.shape, F32),
        ],
        in_specs=[whole(SMEM)] + [whole()] * 7 + [whole(pltpu.HBM)],
        out_specs=[whole(pltpu.HBM), whole(pltpu.HBM)],
        scratch_shapes=[
            VMEM((n * TILE, table.shape[1]), F32),
            VMEM(accum.shape, F32),
            pltpu.SemaphoreType.DMA,
            pltpu.SemaphoreType.DMA((n,)),
        ],
        input_output_aliases={8: 0},
        compiler_params=params(),
    )(blocks, last, *sums, old, table, accum, target)


def after(x, *earlier):
    return lax.optimization_barrier((x,) + earlier)[0]


def gathered(pooled_grad, send_sample, send_row, send_count, union_blocks, table, accum):
    shards = lax.axis_size("shard")
    reps = lax.axis_size("rep")
    cap = send_sample.shape[1]
    span = union_blocks.shape[1] * TILE
    old_accum = accum.reshape(-1, TILE)

    def swap(x, flip):
        pairs = []
        for z in range(shards):
            for r in range(reps):
                dz, dr = flip(r)
                pairs.append((z * reps + r, (z ^ dz) * reps + (r ^ dr)))
        return lax.ppermute(x, ("shard", "rep"), pairs)

    def first(x):
        return swap(x, lambda r: (0, 2 if r % 2 == 0 else 4))

    def second(x):
        return swap(x, lambda r: (0, 4 if r % 2 == 0 else 2))

    def core(x):
        return swap(x, lambda r: (0, 1))

    mine = pack(send_count, pooled_grad, send_sample, send_row)
    table = load(after(table, mine[0]))
    arrived = [swap(mine[j], lambda r: (j, 0)) for j in (2, 3, 1)]
    own = join(after(mine[0], table), *arrived)
    one = first(own)
    own_c = core(own)
    part, old, target = own_sum(union_blocks, own, old_accum, table, span, cap)
    two = second(after(own, part, own_c))
    diag = second(one)
    near, side, part_c = sum_call(near_kernel, [one, two, own_c], [part], 3, span, cap)
    one_c, two_c = core(one), core(two)
    last = core(after(diag, near))
    mine, near_c, side_c = sum_call(
        rest_kernel, [diag, one_c, two_c], [near, side, part_c], 3, span, cap
    )
    table_out, accum_out = update(
        union_blocks, last, (mine, near_c, side_c), old, table, old_accum, target, cap
    )
    return table_out, accum_out.reshape(accum.shape)


def reduced(pooled_grad, send_sample, send_row, send_count, union_blocks, table, accum):
    columns = pooled_grad.shape[1]
    samples = pooled_grad.shape[0]
    active = (lax.broadcasted_iota(jnp.int32, send_sample.shape, 1) < send_count[:, None]).astype(F32)
    lengths = jax.ops.segment_sum(active.reshape(-1), send_sample.reshape(-1), num_segments=samples)
    scaled = active / jnp.maximum(lengths, 1.0)[send_sample]
    values = (pooled_grad[send_sample].astype(F32) * scaled[:, :, None]).astype(BF16)
    arrived = lax.all_to_all(values, "shard", split_axis=0, concat_axis=0, tiled=True)
    places = lax.all_to_all(send_row, "shard", split_axis=0, concat_axis=0, tiled=True)
    blocks = union_blocks[0]
    span = blocks.shape[0] * TILE
    local = (
        jnp.zeros((span, columns), F32)
        .at[places.reshape(-1)]
        .add(arrived.reshape(-1, columns).astype(F32))
    )
    table_tiles = table.reshape(-1, TILE, columns)
    accum_tiles = accum.reshape(-1, TILE)
    grad = lax.optimization_barrier(lax.psum(local.astype(BF16), "rep")).astype(F32)
    acc_new = accum_tiles[blocks].reshape(span) + jnp.mean(grad * grad, axis=-1)
    rows_new = table_tiles[blocks].reshape(span, columns) - LEARNING_RATE * grad / (
        jnp.sqrt(acc_new)[:, None] + EPSILON
    )
    table_out = table_tiles.at[blocks].set(rows_new.reshape(-1, TILE, columns)).reshape(table.shape)
    accum_out = accum_tiles.at[blocks].set(acc_new.reshape(-1, TILE)).reshape(accum.shape)
    return table_out, accum_out


def solution(mesh):
    both = ("shard", "rep")
    in_specs = (
        P(both, None),
        P(both, None),
        P(both, None),
        P(both),
        P("shard", None),
        P("shard", None),
        P("shard"),
    )
    out_specs = (P("shard", None), P("shard"))
    small = mesh.shape["shard"] == 4 and mesh.shape["rep"] == 8
    return jax.shard_map(
        gathered if small else reduced,
        mesh=mesh,
        in_specs=in_specs,
        out_specs=out_specs,
        check_vma=False,
    )
```

```python
import functools

import jax
import jax.numpy as jnp
from jax import lax
from jax.experimental import pallas as pl
from jax.experimental.pallas import tpu as pltpu
from jax.sharding import PartitionSpec as P

TILE = 128
LOAD_MIB = 56
PACK_BYTES = 60 * 1024 * 1024
TAIL = 16
LEARNING_RATE = 0.5
EPSILON = 1e-06
VMEM = pltpu.VMEM
SMEM = pltpu.SMEM
F32 = jnp.float32
BF16 = jnp.bfloat16


def params(mib=24):
    return pltpu.CompilerParams(vmem_limit_bytes=mib * 2**20)


def whole(space=VMEM):
    return pl.BlockSpec(memory_space=space)


def pack_kernel(count_in, grad_in, sample_in, row_in, *refs):
    *out_refs, count_ref, grad_ref, sample_ref, row_ref, sems = refs
    copies = [
        pltpu.make_async_copy(src, dst, sems.at[i])
        for i, (src, dst) in enumerate(
            (
                (sample_in, sample_ref),
                (count_in, count_ref),
                (grad_in, grad_ref),
                (row_in, row_ref),
            )
        )
    ]
    for c in copies:
        c.start()
    owners = len(out_refs)
    cap = sample_ref.shape[1]
    samples, cols = grad_ref.shape
    me = lax.axis_index("shard")
    lane = lax.broadcasted_iota(jnp.int32, (1, cap), 1)
    sub = lax.broadcasted_iota(jnp.int32, (samples, cap), 0)

    def picks(o):
        live = jnp.where(lane < count_ref[o], sample_ref[pl.ds(o, 1), :], -1)
        return (sub == live).astype(F32)

    copies[0].wait()
    copies[1].wait()
    total = picks(0)
    for o in range(1, owners):
        total = total + picks(o)
    lengths = jnp.sum(total, axis=1, keepdims=True)
    copies[2].wait()
    scaled = (grad_ref[...].astype(F32) * (1.0 / jnp.maximum(lengths, 1.0))).astype(BF16)
    copies[3].wait()
    tail_row = lax.broadcasted_iota(jnp.int32, (TAIL, cap), 0)
    for j in range(owners):
        o = me ^ j
        values = lax.dot_general(
            picks(o).astype(BF16), scaled, (((0,), (0,)), ((), ())), preferred_element_type=F32
        )
        out_refs[j][0:cap, :] = values.astype(BF16)
        row = row_ref[pl.ds(o, 1), :]
        slot = row // TILE
        within = row - slot * TILE
        tail = jnp.where(tail_row == 0, slot, jnp.where(tail_row == 1, within, 0))
        out_refs[j][cap : cap + TAIL, :] = jnp.zeros((TAIL, cols), BF16)
        out_refs[j][cap : cap + TAIL, 0:cap] = tail.astype(F32).astype(BF16)


def pack(count, grad, sample, row):
    owners, cap = sample.shape
    shape = VMEM((cap + TAIL, grad.shape[1]), BF16)
    return pl.pallas_call(
        pack_kernel,
        out_shape=[shape] * owners,
        in_specs=[whole(pltpu.HBM)] * 4,
        out_specs=[whole()] * owners,
        scratch_shapes=[
            SMEM(count.shape, jnp.int32),
            VMEM(grad.shape, BF16),
            VMEM(sample.shape, jnp.int32),
            VMEM(row.shape, jnp.int32),
            pltpu.SemaphoreType.DMA((4,)),
        ],
        compiler_params=pltpu.CompilerParams(vmem_limit_bytes=PACK_BYTES),
    )(count, grad, sample, row)


def tiny(cols):
    return pl.CostEstimate(flops=cols, bytes_accessed=cols, transcendentals=0)


def join_kernel(*refs):
    *payloads, out = refs
    cols = out.shape[1]
    sub = lax.broadcasted_iota(jnp.int32, (TAIL, cols), 0)
    tail = jnp.zeros((TAIL, cols), F32)
    at = 0
    for ref in payloads:
        rows = ref.shape[0] - TAIL
        out[at : at + rows, :] = ref[0:rows, :]
        own = ref[rows : rows + TAIL, :].astype(F32)
        for i in range(2 * (rows // TILE)):
            tail = jnp.where(sub == 2 * (at // TILE) + i, own[i : i + 1, :], tail)
        at += rows
    out[at : at + TAIL, :] = tail.astype(BF16)


def join(*payloads):
    cols = payloads[0].shape[1]
    rows = sum(p.shape[0] - TAIL for p in payloads) + TAIL
    return pl.pallas_call(
        join_kernel,
        out_shape=jax.ShapeDtypeStruct((rows, cols), BF16),
        in_specs=[whole()] * len(payloads),
        out_specs=whole(),
        compiler_params=params(),
        cost_estimate=tiny(cols),
    )(*payloads)


def positions(ref, cap):
    entries = ref.shape[0] - TAIL
    tail = ref[entries : entries + TAIL, 0:cap].astype(F32)
    n = entries // cap
    slot = jnp.concatenate([tail[2 * c : 2 * c + 1] for c in range(n)], axis=1)
    within = jnp.concatenate([tail[2 * c + 1 : 2 * c + 2] for c in range(n)], axis=1)
    return slot, within


def block_sum(ref, place, k):
    slot, within = place
    here = jnp.where(slot == k, within, -1.0).astype(BF16)
    entries = here.shape[1]
    sub = lax.broadcasted_iota(jnp.int32, (TILE, entries), 0).astype(F32).astype(BF16)
    pick = jnp.where(sub == here, jnp.ones((), BF16), jnp.zeros((), BF16))
    return jnp.dot(pick, ref[0:entries, :], preferred_element_type=F32)


def group_sum(ref, place, k, size):
    slot, within = place
    entries = slot.shape[1]
    sub = lax.broadcasted_iota(jnp.int32, (TILE, entries), 0).astype(F32).astype(BF16)
    picks = []
    for b in range(k, k + size):
        here = jnp.where(slot == b, within, -1.0).astype(BF16)
        picks.append(jnp.where(sub == here, jnp.ones((), BF16), jnp.zeros((), BF16)))
    pick = jnp.concatenate(picks, axis=0)
    return jnp.dot(pick, ref[0:entries, :], preferred_element_type=F32)


def tile(ref, block):
    return ref.at[pl.ds(pl.multiple_of(block * TILE, TILE), TILE), :]


CHUNKS = 4


def load_kernel(blocks_ref, table_in, table_out, table_ref, loads, kept):
    n = blocks_ref.shape[1]
    tiles = table_in.shape[0] // TILE
    size = tiles // CHUNKS
    copies = []
    for i in range(CHUNKS):
        rows = pl.ds(i * size * TILE, size * TILE)
        c = pltpu.make_async_copy(table_in.at[rows, :], table_out.at[rows, :], loads.at[i])
        c.start()
        copies.append(c)
    seen = jnp.int32(0)
    for i in range(CHUNKS):
        copies[i].wait()
        for t in range(i * size, (i + 1) * size):
            touched = blocks_ref[0, jnp.minimum(seen, n - 1)] == t

            @pl.when(jnp.logical_not(touched))
            def _():
                pltpu.make_async_copy(tile(table_out, t), tile(table_ref, t), kept).start()

            seen = seen + touched.astype(jnp.int32)
    for _ in range(tiles - n):
        pltpu.make_async_copy(tile(table_out, 0), tile(table_ref, 0), kept).wait()


def load(blocks, table):
    return pl.pallas_call(
        load_kernel,
        out_shape=[VMEM(table.shape, F32), jax.ShapeDtypeStruct(table.shape, F32)],
        in_specs=[whole(SMEM), whole(pltpu.HBM)],
        out_specs=[whole(), whole(pltpu.HBM)],
        scratch_shapes=[pltpu.SemaphoreType.DMA((CHUNKS,)), pltpu.SemaphoreType.DMA],
        compiler_params=params(LOAD_MIB),
        cost_estimate=pl.CostEstimate(
            flops=0, bytes_accessed=4 * table.size * 3, transcendentals=0
        ),
    )(blocks, table)


def own_kernel(cap, blocks_ref, own, accum_ref, part, old):
    place = positions(own, cap)
    for k in range(part.shape[0] // TILE):
        span = slice(k * TILE, (k + 1) * TILE)
        part[span, :] = block_sum(own, place, k)
        row = accum_ref[pl.ds(blocks_ref[0, k], 1), :]
        old[span, :] = jnp.broadcast_to(row, (TILE, TILE)).T


def own_sum(blocks, own, accum, span, cap):
    entries, cols = own.shape[0] - TAIL, own.shape[1]
    return pl.pallas_call(
        functools.partial(own_kernel, cap),
        out_shape=[
            jax.ShapeDtypeStruct((span, cols), F32),
            jax.ShapeDtypeStruct((span, TILE), F32),
        ],
        in_specs=[whole(SMEM), whole(), whole()],
        out_specs=[whole()] * 2,
        compiler_params=params(),
        cost_estimate=pl.CostEstimate(
            flops=2 * span * entries * cols, bytes_accessed=span * cols * 4, transcendentals=0
        ),
    )(blocks, own, accum)


def near_kernel(cap, one, two, own_c, part, near, side, part_c):
    places = [positions(ref, cap) for ref in (one, two, own_c)]
    for k in range(0, near.shape[0] // TILE, 4):
        span = slice(k * TILE, (k + 4) * TILE)
        near[span, :] = part[span, :] + group_sum(one, places[0], k, 4)
        side[span, :] = group_sum(two, places[1], k, 4)
        part_c[span, :] = group_sum(own_c, places[2], k, 4)


def rest_kernel(cap, diag, one_c, two_c, near, side, part_c, mine, near_c, side_c):
    places = [positions(ref, cap) for ref in (diag, one_c, two_c)]
    for k in range(0, near.shape[0] // TILE, 4):
        span = slice(k * TILE, (k + 4) * TILE)
        mine[span, :] = near[span, :] + (side[span, :] + group_sum(diag, places[0], k, 4))
        near_c[span, :] = part_c[span, :] + group_sum(one_c, places[1], k, 4)
        side_c[span, :] = group_sum(two_c, places[2], k, 4)


def sum_call(kernel, payloads, parts, results, span, cap):
    entries, cols = payloads[0].shape[0] - TAIL, payloads[0].shape[1]
    wide = jax.ShapeDtypeStruct((span, cols), F32)
    return pl.pallas_call(
        functools.partial(kernel, cap),
        out_shape=[wide] * results,
        in_specs=[whole()] * (len(payloads) + len(parts)),
        out_specs=[whole()] * results,
        compiler_params=params(),
        cost_estimate=pl.CostEstimate(
            flops=2 * span * entries * cols * len(payloads),
            bytes_accessed=span * cols * 4 * (results + len(parts)),
            transcendentals=0,
        ),
    )(*payloads, *parts)


def update_kernel(
    cap, blocks_ref, last, mine, near, side, old, table_in, accum_ref, alias,
    table_ref, accum_out, rows_out, accum_new, sem, sems,
):
    del alias
    n = rows_out.shape[0] // TILE
    cols = rows_out.shape[1]
    place = positions(last, cap)
    accum_new[...] = accum_ref[...]
    diagonal = lax.broadcasted_iota(jnp.int32, (TILE, TILE), 0) == lax.broadcasted_iota(
        jnp.int32, (TILE, TILE), 1
    )
    ones = jnp.ones((2 * cols, TILE), BF16)
    news = []
    copies = []
    for g in range(0, n, 4):
        span = slice(g * TILE, (g + 4) * TILE)
        other = near[span, :] + (side[span, :] + group_sum(last, place, g, 4))
        grad = (mine[span, :] + other).astype(BF16).astype(F32)
        square = grad * grad
        high = square.astype(BF16)
        low = (square - high.astype(F32)).astype(BF16)
        total = jnp.dot(jnp.concatenate([high, low], axis=1), ones, preferred_element_type=F32)
        new = old[span, :] + total * (1.0 / cols)
        rate = LEARNING_RATE / (jnp.sqrt(new) + EPSILON)
        for k in range(g, g + 4):
            block = pl.multiple_of(blocks_ref[0, k] * TILE, TILE)
            at = slice((k - g) * TILE, (k - g + 1) * TILE)
            here = slice(k * TILE, (k + 1) * TILE)
            for c in range(0, cols, TILE):
                rows_out[here, c : c + TILE] = (
                    table_in[pl.ds(block, TILE), c : c + TILE] - grad[at, c : c + TILE] * rate[at, :]
                )
            news.append(jnp.sum(jnp.where(diagonal, new[at, :], 0.0), axis=0, keepdims=True))
            c = pltpu.make_async_copy(rows_out.at[here, :], tile(table_ref, blocks_ref[0, k]), sems.at[k])
            c.start()
            copies.append(c)
    for k in range(n):
        accum_new[pl.ds(blocks_ref[0, k], 1), :] = news[k]
    c = pltpu.make_async_copy(accum_new, accum_out, sem)
    c.start()
    for c in copies + [c]:
        c.wait()


def update(blocks, last, sums, old, table, accum, target, cap):
    n = blocks.shape[1]
    return pl.pallas_call(
        functools.partial(update_kernel, cap),
        out_shape=[
            jax.ShapeDtypeStruct(table.shape, F32),
            jax.ShapeDtypeStruct(accum.shape, F32),
        ],
        in_specs=[whole(SMEM)] + [whole()] * 7 + [whole(pltpu.HBM)],
        out_specs=[whole(pltpu.HBM), whole(pltpu.HBM)],
        scratch_shapes=[
            VMEM((n * TILE, table.shape[1]), F32),
            VMEM(accum.shape, F32),
            pltpu.SemaphoreType.DMA,
            pltpu.SemaphoreType.DMA((n,)),
        ],
        input_output_aliases={8: 0},
        compiler_params=params(),
    )(blocks, last, *sums, old, table, accum, target)


def after(x, *earlier):
    return lax.optimization_barrier((x,) + earlier)[0]


def gathered(pooled_grad, send_sample, send_row, send_count, union_blocks, table, accum):
    shards = lax.axis_size("shard")
    reps = lax.axis_size("rep")
    cap = send_sample.shape[1]
    span = union_blocks.shape[1] * TILE
    old_accum = accum.reshape(-1, TILE)

    def swap(x, flip):
        pairs = []
        for z in range(shards):
            for r in range(reps):
                dz, dr = flip(r)
                pairs.append((z * reps + r, (z ^ dz) * reps + (r ^ dr)))
        return lax.ppermute(x, ("shard", "rep"), pairs)

    def first(x):
        return swap(x, lambda r: (0, 2 if r % 2 == 0 else 4))

    def second(x):
        return swap(x, lambda r: (0, 4 if r % 2 == 0 else 2))

    def core(x):
        return swap(x, lambda r: (0, 1))

    mine = pack(send_count, pooled_grad, send_sample, send_row)
    table, target = load(union_blocks, after(table, mine[0]))
    arrived = [swap(mine[j], lambda r: (j, 0)) for j in (2, 3, 1)]
    early = first(mine[0])
    own = join(after(mine[0], table), *arrived)
    one = join(early, first(join(*arrived)))
    own_c = core(after(own, early))
    part, old = own_sum(union_blocks, own, old_accum, span, cap)
    two = second(after(own, part, own_c))
    diag = second(one)
    near, side, part_c = sum_call(near_kernel, [one, two, own_c], [part], 3, span, cap)
    one_c, two_c = core(one), core(two)
    last = core(after(diag, near))
    mine, near_c, side_c = sum_call(
        rest_kernel, [diag, one_c, two_c], [near, side, part_c], 3, span, cap
    )
    table_out, accum_out = update(
        union_blocks, last, (mine, near_c, side_c), old, table, old_accum, target, cap
    )
    return table_out, accum_out.reshape(accum.shape)


def reduced(pooled_grad, send_sample, send_row, send_count, union_blocks, table, accum):
    columns = pooled_grad.shape[1]
    samples = pooled_grad.shape[0]
    active = (lax.broadcasted_iota(jnp.int32, send_sample.shape, 1) < send_count[:, None]).astype(F32)
    lengths = jax.ops.segment_sum(active.reshape(-1), send_sample.reshape(-1), num_segments=samples)
    scaled = active / jnp.maximum(lengths, 1.0)[send_sample]
    values = (pooled_grad[send_sample].astype(F32) * scaled[:, :, None]).astype(BF16)
    arrived = lax.all_to_all(values, "shard", split_axis=0, concat_axis=0, tiled=True)
    places = lax.all_to_all(send_row, "shard", split_axis=0, concat_axis=0, tiled=True)
    blocks = union_blocks[0]
    span = blocks.shape[0] * TILE
    local = (
        jnp.zeros((span, columns), F32)
        .at[places.reshape(-1)]
        .add(arrived.reshape(-1, columns).astype(F32))
    )
    table_tiles = table.reshape(-1, TILE, columns)
    accum_tiles = accum.reshape(-1, TILE)
    grad = lax.optimization_barrier(lax.psum(local.astype(BF16), "rep")).astype(F32)
    acc_new = accum_tiles[blocks].reshape(span) + jnp.mean(grad * grad, axis=-1)
    rows_new = table_tiles[blocks].reshape(span, columns) - LEARNING_RATE * grad / (
        jnp.sqrt(acc_new)[:, None] + EPSILON
    )
    table_out = table_tiles.at[blocks].set(rows_new.reshape(-1, TILE, columns)).reshape(table.shape)
    accum_out = accum_tiles.at[blocks].set(acc_new.reshape(-1, TILE)).reshape(accum.shape)
    return table_out, accum_out


def solution(mesh):
    both = ("shard", "rep")
    in_specs = (
        P(both, None),
        P(both, None),
        P(both, None),
        P(both),
        P("shard", None),
        P("shard", None),
        P("shard"),
    )
    out_specs = (P("shard", None), P("shard"))
    small = mesh.shape["shard"] == 4 and mesh.shape["rep"] == 8
    return jax.shard_map(
        gathered if small else reduced,
        mesh=mesh,
        in_specs=in_specs,
        out_specs=out_specs,
        check_vma=False,
    )
```

```python
import functools

import jax
import jax.numpy as jnp
from jax import lax
from jax.experimental import pallas as pl
from jax.experimental.pallas import tpu as pltpu
from jax.sharding import PartitionSpec as P

TILE = 128
LOAD_MIB = 56
PACK_BYTES = 60 * 1024 * 1024
TAIL = 16
LEARNING_RATE = 0.5
EPSILON = 1e-06
VMEM = pltpu.VMEM
SMEM = pltpu.SMEM
F32 = jnp.float32
BF16 = jnp.bfloat16


def params(mib=24):
    return pltpu.CompilerParams(vmem_limit_bytes=mib * 2**20)


def whole(space=VMEM):
    return pl.BlockSpec(memory_space=space)


def pack_kernel(count_in, grad_in, sample_in, row_in, *refs):
    *out_refs, count_ref, grad_ref, sample_ref, row_ref, sems = refs
    copies = [
        pltpu.make_async_copy(src, dst, sems.at[i])
        for i, (src, dst) in enumerate(
            (
                (sample_in, sample_ref),
                (count_in, count_ref),
                (grad_in, grad_ref),
                (row_in, row_ref),
            )
        )
    ]
    for c in copies:
        c.start()
    owners = len(out_refs)
    cap = sample_ref.shape[1]
    samples, cols = grad_ref.shape
    me = lax.axis_index("shard")
    lane = lax.broadcasted_iota(jnp.int32, (1, cap), 1)
    sub = lax.broadcasted_iota(jnp.int32, (samples, cap), 0)

    def picks(o):
        live = jnp.where(lane < count_ref[o], sample_ref[pl.ds(o, 1), :], -1)
        return (sub == live).astype(F32)

    copies[0].wait()
    copies[1].wait()
    total = picks(0)
    for o in range(1, owners):
        total = total + picks(o)
    lengths = jnp.sum(total, axis=1, keepdims=True)
    copies[2].wait()
    scaled = (grad_ref[...].astype(F32) * (1.0 / jnp.maximum(lengths, 1.0))).astype(BF16)
    copies[3].wait()
    tail_row = lax.broadcasted_iota(jnp.int32, (TAIL, cap), 0)
    for j in range(owners):
        o = me ^ j
        values = lax.dot_general(
            picks(o).astype(BF16), scaled, (((0,), (0,)), ((), ())), preferred_element_type=F32
        )
        out_refs[j][0:cap, :] = values.astype(BF16)
        row = row_ref[pl.ds(o, 1), :]
        slot = row // TILE
        within = row - slot * TILE
        tail = jnp.where(tail_row == 0, slot, jnp.where(tail_row == 1, within, 0))
        out_refs[j][cap : cap + TAIL, :] = jnp.zeros((TAIL, cols), BF16)
        out_refs[j][cap : cap + TAIL, 0:cap] = tail.astype(F32).astype(BF16)


def pack(count, grad, sample, row):
    owners, cap = sample.shape
    shape = VMEM((cap + TAIL, grad.shape[1]), BF16)
    return pl.pallas_call(
        pack_kernel,
        out_shape=[shape] * owners,
        in_specs=[whole(pltpu.HBM)] * 4,
        out_specs=[whole()] * owners,
        scratch_shapes=[
            SMEM(count.shape, jnp.int32),
            VMEM(grad.shape, BF16),
            VMEM(sample.shape, jnp.int32),
            VMEM(row.shape, jnp.int32),
            pltpu.SemaphoreType.DMA((4,)),
        ],
        compiler_params=pltpu.CompilerParams(vmem_limit_bytes=PACK_BYTES),
    )(count, grad, sample, row)


def tiny(cols):
    return pl.CostEstimate(flops=cols, bytes_accessed=cols, transcendentals=0)


def join_kernel(*refs):
    *payloads, out = refs
    cols = out.shape[1]
    sub = lax.broadcasted_iota(jnp.int32, (TAIL, cols), 0)
    tail = jnp.zeros((TAIL, cols), F32)
    at = 0
    for ref in payloads:
        rows = ref.shape[0] - TAIL
        out[at : at + rows, :] = ref[0:rows, :]
        own = ref[rows : rows + TAIL, :].astype(F32)
        for i in range(2 * (rows // TILE)):
            tail = jnp.where(sub == 2 * (at // TILE) + i, own[i : i + 1, :], tail)
        at += rows
    out[at : at + TAIL, :] = tail.astype(BF16)


def join(*payloads):
    cols = payloads[0].shape[1]
    rows = sum(p.shape[0] - TAIL for p in payloads) + TAIL
    return pl.pallas_call(
        join_kernel,
        out_shape=jax.ShapeDtypeStruct((rows, cols), BF16),
        in_specs=[whole()] * len(payloads),
        out_specs=whole(),
        compiler_params=params(),
        cost_estimate=tiny(cols),
    )(*payloads)


def positions(ref, cap):
    entries = ref.shape[0] - TAIL
    tail = ref[entries : entries + TAIL, 0:cap].astype(F32)
    n = entries // cap
    slot = jnp.concatenate([tail[2 * c : 2 * c + 1] for c in range(n)], axis=1)
    within = jnp.concatenate([tail[2 * c + 1 : 2 * c + 2] for c in range(n)], axis=1)
    return slot, within


def block_sum(ref, place, k):
    slot, within = place
    here = jnp.where(slot == k, within, -1.0).astype(BF16)
    entries = here.shape[1]
    sub = lax.broadcasted_iota(jnp.int32, (TILE, entries), 0).astype(F32).astype(BF16)
    pick = jnp.where(sub == here, jnp.ones((), BF16), jnp.zeros((), BF16))
    return jnp.dot(pick, ref[0:entries, :], preferred_element_type=F32)


def group_sum(ref, place, k, size):
    slot, within = place
    entries = slot.shape[1]
    sub = lax.broadcasted_iota(jnp.int32, (TILE, entries), 0).astype(F32).astype(BF16)
    picks = []
    for b in range(k, k + size):
        here = jnp.where(slot == b, within, -1.0).astype(BF16)
        picks.append(jnp.where(sub == here, jnp.ones((), BF16), jnp.zeros((), BF16)))
    pick = jnp.concatenate(picks, axis=0)
    return jnp.dot(pick, ref[0:entries, :], preferred_element_type=F32)


def tile(ref, block):
    return ref.at[pl.ds(pl.multiple_of(block * TILE, TILE), TILE), :]


CHUNKS = 4


def load_kernel(blocks_ref, table_in, table_out, table_ref, loads, kept):
    n = blocks_ref.shape[1]
    tiles = table_in.shape[0] // TILE
    size = tiles // CHUNKS
    copies = []
    for i in range(CHUNKS):
        rows = pl.ds(i * size * TILE, size * TILE)
        c = pltpu.make_async_copy(table_in.at[rows, :], table_out.at[rows, :], loads.at[i])
        c.start()
        copies.append(c)
    seen = jnp.int32(0)
    for i in range(CHUNKS):
        copies[i].wait()
        for t in range(i * size, (i + 1) * size):
            touched = blocks_ref[0, jnp.minimum(seen, n - 1)] == t

            @pl.when(jnp.logical_not(touched))
            def _():
                pltpu.make_async_copy(tile(table_out, t), tile(table_ref, t), kept).start()

            seen = seen + touched.astype(jnp.int32)
    for _ in range(tiles - n):
        pltpu.make_async_copy(tile(table_out, 0), tile(table_ref, 0), kept).wait()


def load(blocks, table):
    return pl.pallas_call(
        load_kernel,
        out_shape=[VMEM(table.shape, F32), jax.ShapeDtypeStruct(table.shape, F32)],
        in_specs=[whole(SMEM), whole(pltpu.HBM)],
        out_specs=[whole(), whole(pltpu.HBM)],
        scratch_shapes=[pltpu.SemaphoreType.DMA((CHUNKS,)), pltpu.SemaphoreType.DMA],
        compiler_params=params(LOAD_MIB),
        cost_estimate=pl.CostEstimate(
            flops=0, bytes_accessed=4 * table.size * 3, transcendentals=0
        ),
    )(blocks, table)


def own_kernel(cap, blocks_ref, own, own_c, accum_ref, part, part_c, old):
    places = [positions(ref, cap) for ref in (own, own_c)]
    for k in range(part.shape[0] // TILE):
        span = slice(k * TILE, (k + 1) * TILE)
        part[span, :] = block_sum(own, places[0], k)
        part_c[span, :] = block_sum(own_c, places[1], k)
        row = accum_ref[pl.ds(blocks_ref[0, k], 1), :]
        old[span, :] = jnp.broadcast_to(row, (TILE, TILE)).T


def own_sum(blocks, own, own_c, accum, span, cap):
    entries, cols = own.shape[0] - TAIL, own.shape[1]
    return pl.pallas_call(
        functools.partial(own_kernel, cap),
        out_shape=[
            jax.ShapeDtypeStruct((span, cols), F32),
            jax.ShapeDtypeStruct((span, cols), F32),
            jax.ShapeDtypeStruct((span, TILE), F32),
        ],
        in_specs=[whole(SMEM)] + [whole()] * 3,
        out_specs=[whole()] * 3,
        compiler_params=params(),
        cost_estimate=pl.CostEstimate(
            flops=2 * span * entries * cols, bytes_accessed=span * cols * 4, transcendentals=0
        ),
    )(blocks, own, own_c, accum)


def near_kernel(cap, one, two, one_c, part, part_c, near, side, near_c):
    places = [positions(ref, cap) for ref in (one, two, one_c)]
    for k in range(0, near.shape[0] // TILE, 4):
        span = slice(k * TILE, (k + 4) * TILE)
        near[span, :] = part[span, :] + group_sum(one, places[0], k, 4)
        side[span, :] = group_sum(two, places[1], k, 4)
        near_c[span, :] = part_c[span, :] + group_sum(one_c, places[2], k, 4)


def rest_kernel(cap, diag, two_c, near, side, mine, side_c):
    places = [positions(ref, cap) for ref in (diag, two_c)]
    for k in range(0, near.shape[0] // TILE, 4):
        span = slice(k * TILE, (k + 4) * TILE)
        mine[span, :] = near[span, :] + (side[span, :] + group_sum(diag, places[0], k, 4))
        side_c[span, :] = group_sum(two_c, places[1], k, 4)


def sum_call(kernel, payloads, parts, results, span, cap):
    entries, cols = payloads[0].shape[0] - TAIL, payloads[0].shape[1]
    wide = jax.ShapeDtypeStruct((span, cols), F32)
    return pl.pallas_call(
        functools.partial(kernel, cap),
        out_shape=[wide] * results,
        in_specs=[whole()] * (len(payloads) + len(parts)),
        out_specs=[whole()] * results,
        compiler_params=params(),
        cost_estimate=pl.CostEstimate(
            flops=2 * span * entries * cols * len(payloads),
            bytes_accessed=span * cols * 4 * (results + len(parts)),
            transcendentals=0,
        ),
    )(*payloads, *parts)


def update_kernel(
    cap, blocks_ref, last, mine, near, side, old, table_in, accum_ref, alias,
    table_ref, accum_out, rows_out, accum_new, sem, sems,
):
    del alias
    n = rows_out.shape[0] // TILE
    cols = rows_out.shape[1]
    place = positions(last, cap)
    accum_new[...] = accum_ref[...]
    diagonal = lax.broadcasted_iota(jnp.int32, (TILE, TILE), 0) == lax.broadcasted_iota(
        jnp.int32, (TILE, TILE), 1
    )
    ones = jnp.ones((2 * cols, TILE), BF16)
    news = []
    copies = []
    for g in range(0, n, 4):
        span = slice(g * TILE, (g + 4) * TILE)
        other = near[span, :] + (side[span, :] + group_sum(last, place, g, 4))
        grad = (mine[span, :] + other).astype(BF16).astype(F32)
        square = grad * grad
        high = square.astype(BF16)
        low = (square - high.astype(F32)).astype(BF16)
        total = jnp.dot(jnp.concatenate([high, low], axis=1), ones, preferred_element_type=F32)
        new = old[span, :] + total * (1.0 / cols)
        rate = LEARNING_RATE / (jnp.sqrt(new) + EPSILON)
        for k in range(g, g + 4):
            block = pl.multiple_of(blocks_ref[0, k] * TILE, TILE)
            at = slice((k - g) * TILE, (k - g + 1) * TILE)
            here = slice(k * TILE, (k + 1) * TILE)
            for c in range(0, cols, TILE):
                rows_out[here, c : c + TILE] = (
                    table_in[pl.ds(block, TILE), c : c + TILE] - grad[at, c : c + TILE] * rate[at, :]
                )
            news.append(jnp.sum(jnp.where(diagonal, new[at, :], 0.0), axis=0, keepdims=True))
            c = pltpu.make_async_copy(rows_out.at[here, :], tile(table_ref, blocks_ref[0, k]), sems.at[k])
            c.start()
            copies.append(c)
    for k in range(n):
        accum_new[pl.ds(blocks_ref[0, k], 1), :] = news[k]
    c = pltpu.make_async_copy(accum_new, accum_out, sem)
    c.start()
    for c in copies + [c]:
        c.wait()


def update(blocks, last, sums, old, table, accum, target, cap):
    n = blocks.shape[1]
    return pl.pallas_call(
        functools.partial(update_kernel, cap),
        out_shape=[
            jax.ShapeDtypeStruct(table.shape, F32),
            jax.ShapeDtypeStruct(accum.shape, F32),
        ],
        in_specs=[whole(SMEM)] + [whole()] * 7 + [whole(pltpu.HBM)],
        out_specs=[whole(pltpu.HBM), whole(pltpu.HBM)],
        scratch_shapes=[
            VMEM((n * TILE, table.shape[1]), F32),
            VMEM(accum.shape, F32),
            pltpu.SemaphoreType.DMA,
            pltpu.SemaphoreType.DMA((n,)),
        ],
        input_output_aliases={8: 0},
        compiler_params=params(),
    )(blocks, last, *sums, old, table, accum, target)


def after(x, *earlier):
    return lax.optimization_barrier((x,) + earlier)[0]


def gathered(pooled_grad, send_sample, send_row, send_count, union_blocks, table, accum):
    shards = lax.axis_size("shard")
    reps = lax.axis_size("rep")
    cap = send_sample.shape[1]
    span = union_blocks.shape[1] * TILE
    old_accum = accum.reshape(-1, TILE)

    def swap(x, flip):
        pairs = []
        for z in range(shards):
            for r in range(reps):
                dz, dr = flip(r)
                pairs.append((z * reps + r, (z ^ dz) * reps + (r ^ dr)))
        return lax.ppermute(x, ("shard", "rep"), pairs)

    def first(x):
        return swap(x, lambda r: (0, 2 if r % 2 == 0 else 4))

    def second(x):
        return swap(x, lambda r: (0, 4 if r % 2 == 0 else 2))

    def core(x):
        return swap(x, lambda r: (0, 1))

    mine = pack(send_count, pooled_grad, send_sample, send_row)
    table, target = load(union_blocks, after(table, mine[0]))
    arrived = [swap(mine[j], lambda r: (j, 0)) for j in (2, 3, 1)]
    early = first(mine[0])
    own = join(after(mine[0], table), *arrived)
    one = join(early, first(join(*arrived)))
    own_c = core(after(own, early))
    part, part_c, old = own_sum(union_blocks, own, own_c, old_accum, span, cap)
    two = second(after(own, part))
    diag = second(one)
    one_c, two_c = core(one), core(two)
    near, side, near_c = sum_call(near_kernel, [one, two, one_c], [part, part_c], 3, span, cap)
    last = core(after(diag, near))
    mine, side_c = sum_call(rest_kernel, [diag, two_c], [near, side], 2, span, cap)
    table_out, accum_out = update(
        union_blocks, last, (mine, near_c, side_c), old, table, old_accum, target, cap
    )
    return table_out, accum_out.reshape(accum.shape)


def reduced(pooled_grad, send_sample, send_row, send_count, union_blocks, table, accum):
    columns = pooled_grad.shape[1]
    samples = pooled_grad.shape[0]
    active = (lax.broadcasted_iota(jnp.int32, send_sample.shape, 1) < send_count[:, None]).astype(F32)
    lengths = jax.ops.segment_sum(active.reshape(-1), send_sample.reshape(-1), num_segments=samples)
    scaled = active / jnp.maximum(lengths, 1.0)[send_sample]
    values = (pooled_grad[send_sample].astype(F32) * scaled[:, :, None]).astype(BF16)
    arrived = lax.all_to_all(values, "shard", split_axis=0, concat_axis=0, tiled=True)
    places = lax.all_to_all(send_row, "shard", split_axis=0, concat_axis=0, tiled=True)
    blocks = union_blocks[0]
    span = blocks.shape[0] * TILE
    local = (
        jnp.zeros((span, columns), F32)
        .at[places.reshape(-1)]
        .add(arrived.reshape(-1, columns).astype(F32))
    )
    table_tiles = table.reshape(-1, TILE, columns)
    accum_tiles = accum.reshape(-1, TILE)
    grad = lax.optimization_barrier(lax.psum(local.astype(BF16), "rep")).astype(F32)
    acc_new = accum_tiles[blocks].reshape(span) + jnp.mean(grad * grad, axis=-1)
    rows_new = table_tiles[blocks].reshape(span, columns) - LEARNING_RATE * grad / (
        jnp.sqrt(acc_new)[:, None] + EPSILON
    )
    table_out = table_tiles.at[blocks].set(rows_new.reshape(-1, TILE, columns)).reshape(table.shape)
    accum_out = accum_tiles.at[blocks].set(acc_new.reshape(-1, TILE)).reshape(accum.shape)
    return table_out, accum_out


def solution(mesh):
    both = ("shard", "rep")
    in_specs = (
        P(both, None),
        P(both, None),
        P(both, None),
        P(both),
        P("shard", None),
        P("shard", None),
        P("shard"),
    )
    out_specs = (P("shard", None), P("shard"))
    small = mesh.shape["shard"] == 4 and mesh.shape["rep"] == 8
    return jax.shard_map(
        gathered if small else reduced,
        mesh=mesh,
        in_specs=in_specs,
        out_specs=out_specs,
        check_vma=False,
    )
```

```python
import functools

import jax
import jax.numpy as jnp
from jax import lax
from jax.experimental import pallas as pl
from jax.experimental.pallas import tpu as pltpu
from jax.sharding import PartitionSpec as P

TILE = 128
LOAD_MIB = 56
PACK_BYTES = 60 * 1024 * 1024
TAIL = 16
LEARNING_RATE = 0.5
EPSILON = 1e-06
VMEM = pltpu.VMEM
SMEM = pltpu.SMEM
F32 = jnp.float32
BF16 = jnp.bfloat16


def params(mib=24):
    return pltpu.CompilerParams(vmem_limit_bytes=mib * 2**20)


def whole(space=VMEM):
    return pl.BlockSpec(memory_space=space)


def pack_kernel(count_in, grad_in, sample_in, row_in, *refs):
    *out_refs, count_ref, grad_ref, sample_ref, row_ref, sems = refs
    copies = [
        pltpu.make_async_copy(src, dst, sems.at[i])
        for i, (src, dst) in enumerate(
            (
                (sample_in, sample_ref),
                (count_in, count_ref),
                (grad_in, grad_ref),
                (row_in, row_ref),
            )
        )
    ]
    for c in copies:
        c.start()
    owners = len(out_refs)
    cap = sample_ref.shape[1]
    samples, cols = grad_ref.shape
    me = lax.axis_index("shard")
    lane = lax.broadcasted_iota(jnp.int32, (1, cap), 1)
    sub = lax.broadcasted_iota(jnp.int32, (samples, cap), 0)

    def picks(o):
        live = jnp.where(lane < count_ref[o], sample_ref[pl.ds(o, 1), :], -1)
        return (sub == live).astype(F32)

    copies[0].wait()
    copies[1].wait()
    total = picks(0)
    for o in range(1, owners):
        total = total + picks(o)
    lengths = jnp.sum(total, axis=1, keepdims=True)
    copies[2].wait()
    scaled = (grad_ref[...].astype(F32) * (1.0 / jnp.maximum(lengths, 1.0))).astype(BF16)
    copies[3].wait()
    tail_row = lax.broadcasted_iota(jnp.int32, (TAIL, cap), 0)
    for j in range(owners):
        o = me ^ j
        values = lax.dot_general(
            picks(o).astype(BF16), scaled, (((0,), (0,)), ((), ())), preferred_element_type=F32
        )
        out_refs[j][0:cap, :] = values.astype(BF16)
        row = row_ref[pl.ds(o, 1), :]
        slot = row // TILE
        within = row - slot * TILE
        tail = jnp.where(tail_row == 0, slot, jnp.where(tail_row == 1, within, 0))
        out_refs[j][cap : cap + TAIL, :] = jnp.zeros((TAIL, cols), BF16)
        out_refs[j][cap : cap + TAIL, 0:cap] = tail.astype(F32).astype(BF16)


def pack(count, grad, sample, row):
    owners, cap = sample.shape
    shape = VMEM((cap + TAIL, grad.shape[1]), BF16)
    return pl.pallas_call(
        pack_kernel,
        out_shape=[shape] * owners,
        in_specs=[whole(pltpu.HBM)] * 4,
        out_specs=[whole()] * owners,
        scratch_shapes=[
            SMEM(count.shape, jnp.int32),
            VMEM(grad.shape, BF16),
            VMEM(sample.shape, jnp.int32),
            VMEM(row.shape, jnp.int32),
            pltpu.SemaphoreType.DMA((4,)),
        ],
        compiler_params=pltpu.CompilerParams(vmem_limit_bytes=PACK_BYTES),
    )(count, grad, sample, row)


def tiny(cols):
    return pl.CostEstimate(flops=cols, bytes_accessed=cols, transcendentals=0)


def join_kernel(*refs):
    *payloads, out = refs
    cols = out.shape[1]
    sub = lax.broadcasted_iota(jnp.int32, (TAIL, cols), 0)
    tail = jnp.zeros((TAIL, cols), F32)
    at = 0
    for ref in payloads:
        rows = ref.shape[0] - TAIL
        out[at : at + rows, :] = ref[0:rows, :]
        own = ref[rows : rows + TAIL, :].astype(F32)
        for i in range(2 * (rows // TILE)):
            tail = jnp.where(sub == 2 * (at // TILE) + i, own[i : i + 1, :], tail)
        at += rows
    out[at : at + TAIL, :] = tail.astype(BF16)


def join(*payloads):
    cols = payloads[0].shape[1]
    rows = sum(p.shape[0] - TAIL for p in payloads) + TAIL
    return pl.pallas_call(
        join_kernel,
        out_shape=jax.ShapeDtypeStruct((rows, cols), BF16),
        in_specs=[whole()] * len(payloads),
        out_specs=whole(),
        compiler_params=params(),
        cost_estimate=tiny(cols),
    )(*payloads)


def positions(ref, cap):
    entries = ref.shape[0] - TAIL
    tail = ref[entries : entries + TAIL, 0:cap].astype(F32)
    n = entries // cap
    slot = jnp.concatenate([tail[2 * c : 2 * c + 1] for c in range(n)], axis=1)
    within = jnp.concatenate([tail[2 * c + 1 : 2 * c + 2] for c in range(n)], axis=1)
    return slot, within


def block_sum(ref, place, k):
    slot, within = place
    here = jnp.where(slot == k, within, -1.0).astype(BF16)
    entries = here.shape[1]
    sub = lax.broadcasted_iota(jnp.int32, (TILE, entries), 0).astype(F32).astype(BF16)
    pick = jnp.where(sub == here, jnp.ones((), BF16), jnp.zeros((), BF16))
    return jnp.dot(pick, ref[0:entries, :], preferred_element_type=F32)


def group_sum(ref, place, k, size):
    slot, within = place
    entries = slot.shape[1]
    sub = lax.broadcasted_iota(jnp.int32, (TILE, entries), 0).astype(F32).astype(BF16)
    picks = []
    for b in range(k, k + size):
        here = jnp.where(slot == b, within, -1.0).astype(BF16)
        picks.append(jnp.where(sub == here, jnp.ones((), BF16), jnp.zeros((), BF16)))
    pick = jnp.concatenate(picks, axis=0)
    return jnp.dot(pick, ref[0:entries, :], preferred_element_type=F32)


def tile(ref, block):
    return ref.at[pl.ds(pl.multiple_of(block * TILE, TILE), TILE), :]


CHUNKS = 4


def load_kernel(blocks_ref, table_in, table_out, table_ref, loads, kept):
    n = blocks_ref.shape[1]
    tiles = table_in.shape[0] // TILE
    size = tiles // CHUNKS
    copies = []
    for i in range(CHUNKS):
        rows = pl.ds(i * size * TILE, size * TILE)
        c = pltpu.make_async_copy(table_in.at[rows, :], table_out.at[rows, :], loads.at[i])
        c.start()
        copies.append(c)
    seen = jnp.int32(0)
    for i in range(CHUNKS):
        copies[i].wait()
        for t in range(i * size, (i + 1) * size):
            touched = blocks_ref[0, jnp.minimum(seen, n - 1)] == t

            @pl.when(jnp.logical_not(touched))
            def _():
                pltpu.make_async_copy(tile(table_out, t), tile(table_ref, t), kept).start()

            seen = seen + touched.astype(jnp.int32)
    for _ in range(tiles - n):
        pltpu.make_async_copy(tile(table_out, 0), tile(table_ref, 0), kept).wait()


def load(blocks, table):
    return pl.pallas_call(
        load_kernel,
        out_shape=[VMEM(table.shape, F32), jax.ShapeDtypeStruct(table.shape, F32)],
        in_specs=[whole(SMEM), whole(pltpu.HBM)],
        out_specs=[whole(), whole(pltpu.HBM)],
        scratch_shapes=[pltpu.SemaphoreType.DMA((CHUNKS,)), pltpu.SemaphoreType.DMA],
        compiler_params=params(LOAD_MIB),
        cost_estimate=pl.CostEstimate(
            flops=0, bytes_accessed=4 * table.size * 3, transcendentals=0
        ),
    )(blocks, table)


def own_kernel(cap, blocks_ref, own, own_c, accum_ref, part, part_c, old):
    places = [positions(ref, cap) for ref in (own, own_c)]
    for k in range(0, part.shape[0] // TILE, 4):
        span = slice(k * TILE, (k + 4) * TILE)
        part[span, :] = group_sum(own, places[0], k, 4)
        part_c[span, :] = group_sum(own_c, places[1], k, 4)
    for k in range(part.shape[0] // TILE):
        row = accum_ref[pl.ds(blocks_ref[0, k], 1), :]
        old[k * TILE : (k + 1) * TILE, :] = jnp.broadcast_to(row, (TILE, TILE)).T


def own_sum(blocks, own, own_c, accum, span, cap):
    entries, cols = own.shape[0] - TAIL, own.shape[1]
    return pl.pallas_call(
        functools.partial(own_kernel, cap),
        out_shape=[
            jax.ShapeDtypeStruct((span, cols), F32),
            jax.ShapeDtypeStruct((span, cols), F32),
            jax.ShapeDtypeStruct((span, TILE), F32),
        ],
        in_specs=[whole(SMEM)] + [whole()] * 3,
        out_specs=[whole()] * 3,
        compiler_params=params(),
        cost_estimate=pl.CostEstimate(
            flops=2 * span * entries * cols, bytes_accessed=span * cols * 4, transcendentals=0
        ),
    )(blocks, own, own_c, accum)


def near_kernel(cap, one, two, one_c, part, part_c, near, side, near_c):
    places = [positions(ref, cap) for ref in (one, two, one_c)]
    for k in range(0, near.shape[0] // TILE, 4):
        span = slice(k * TILE, (k + 4) * TILE)
        near[span, :] = part[span, :] + group_sum(one, places[0], k, 4)
        side[span, :] = group_sum(two, places[1], k, 4)
        near_c[span, :] = part_c[span, :] + group_sum(one_c, places[2], k, 4)


def rest_kernel(cap, diag, two_c, near, side, mine, side_c):
    places = [positions(ref, cap) for ref in (diag, two_c)]
    for k in range(0, near.shape[0] // TILE, 4):
        span = slice(k * TILE, (k + 4) * TILE)
        mine[span, :] = near[span, :] + (side[span, :] + group_sum(diag, places[0], k, 4))
        side_c[span, :] = group_sum(two_c, places[1], k, 4)


def sum_call(kernel, payloads, parts, results, span, cap):
    entries, cols = payloads[0].shape[0] - TAIL, payloads[0].shape[1]
    wide = jax.ShapeDtypeStruct((span, cols), F32)
    return pl.pallas_call(
        functools.partial(kernel, cap),
        out_shape=[wide] * results,
        in_specs=[whole()] * (len(payloads) + len(parts)),
        out_specs=[whole()] * results,
        compiler_params=params(),
        cost_estimate=pl.CostEstimate(
            flops=2 * span * entries * cols * len(payloads),
            bytes_accessed=span * cols * 4 * (results + len(parts)),
            transcendentals=0,
        ),
    )(*payloads, *parts)


def update_kernel(
    cap, blocks_ref, last, mine, near, side, old, table_in, accum_ref, alias,
    table_ref, accum_out, rows_out, accum_new, sem, sems,
):
    del alias
    n = rows_out.shape[0] // TILE
    cols = rows_out.shape[1]
    place = positions(last, cap)
    accum_new[...] = accum_ref[...]
    diagonal = lax.broadcasted_iota(jnp.int32, (TILE, TILE), 0) == lax.broadcasted_iota(
        jnp.int32, (TILE, TILE), 1
    )
    ones = jnp.ones((2 * TILE, TILE), BF16)
    news = []
    copies = []
    bounds = sorted({0, n // 2, 3 * n // 4, n})
    for g, end in zip(bounds, bounds[1:]):
        span = slice(g * TILE, end * TILE)
        other = near[span, :] + (side[span, :] + group_sum(last, place, g, end - g))
        grad = (mine[span, :] + other).astype(BF16).astype(F32)
        square = grad * grad
        square = sum(square[:, c : c + TILE] for c in range(0, cols, TILE))
        high = square.astype(BF16)
        low = (square - high.astype(F32)).astype(BF16)
        total = jnp.dot(jnp.concatenate([high, low], axis=1), ones, preferred_element_type=F32)
        new = old[span, :] + total * (1.0 / cols)
        rate = LEARNING_RATE / (new * lax.rsqrt(new) + EPSILON)
        for k in range(g, end):
            block = pl.multiple_of(blocks_ref[0, k] * TILE, TILE)
            at = slice((k - g) * TILE, (k - g + 1) * TILE)
            here = slice(k * TILE, (k + 1) * TILE)
            for c in range(0, cols, TILE):
                rows_out[here, c : c + TILE] = (
                    table_in[pl.ds(block, TILE), c : c + TILE] - grad[at, c : c + TILE] * rate[at, :]
                )
            news.append(jnp.sum(jnp.where(diagonal, new[at, :], 0.0), axis=0, keepdims=True))
            c = pltpu.make_async_copy(rows_out.at[here, :], tile(table_ref, blocks_ref[0, k]), sems.at[k])
            c.start()
            copies.append(c)
    for k in range(n):
        accum_new[pl.ds(blocks_ref[0, k], 1), :] = news[k]
    c = pltpu.make_async_copy(accum_new, accum_out, sem)
    c.start()
    for c in copies + [c]:
        c.wait()


def update(blocks, last, sums, old, table, accum, target, cap):
    n = blocks.shape[1]
    return pl.pallas_call(
        functools.partial(update_kernel, cap),
        out_shape=[
            jax.ShapeDtypeStruct(table.shape, F32),
            jax.ShapeDtypeStruct(accum.shape, F32),
        ],
        in_specs=[whole(SMEM)] + [whole()] * 7 + [whole(pltpu.HBM)],
        out_specs=[whole(pltpu.HBM), whole(pltpu.HBM)],
        scratch_shapes=[
            VMEM((n * TILE, table.shape[1]), F32),
            VMEM(accum.shape, F32),
            pltpu.SemaphoreType.DMA,
            pltpu.SemaphoreType.DMA((n,)),
        ],
        input_output_aliases={8: 0},
        compiler_params=params(),
    )(blocks, last, *sums, old, table, accum, target)


def after(x, *earlier):
    return lax.optimization_barrier((x,) + earlier)[0]


def gathered(pooled_grad, send_sample, send_row, send_count, union_blocks, table, accum):
    shards = lax.axis_size("shard")
    reps = lax.axis_size("rep")
    cap = send_sample.shape[1]
    span = union_blocks.shape[1] * TILE
    old_accum = accum.reshape(-1, TILE)

    def swap(x, flip):
        pairs = []
        for z in range(shards):
            for r in range(reps):
                dz, dr = flip(r)
                pairs.append((z * reps + r, (z ^ dz) * reps + (r ^ dr)))
        return lax.ppermute(x, ("shard", "rep"), pairs)

    def first(x):
        return swap(x, lambda r: (0, 2 if r % 2 == 0 else 4))

    def second(x):
        return swap(x, lambda r: (0, 4 if r % 2 == 0 else 2))

    def core(x):
        return swap(x, lambda r: (0, 1))

    mine = pack(send_count, pooled_grad, send_sample, send_row)
    table, target = load(union_blocks, after(table, mine[0]))
    arrived = [swap(mine[j], lambda r: (j, 0)) for j in (2, 3, 1)]
    early = first(mine[0])
    own = join(after(mine[0], table), *arrived)
    one = join(early, first(join(*arrived)))
    own_c = core(after(own, early))
    part, part_c, old = own_sum(union_blocks, own, own_c, old_accum, span, cap)
    two = second(after(own, part))
    diag = second(one)
    one_c, two_c = core(one), core(two)
    near, side, near_c = sum_call(near_kernel, [one, two, one_c], [part, part_c], 3, span, cap)
    last = core(after(diag, near))
    mine, side_c = sum_call(rest_kernel, [diag, two_c], [near, side], 2, span, cap)
    table_out, accum_out = update(
        union_blocks, last, (mine, near_c, side_c), old, table, old_accum, target, cap
    )
    return table_out, accum_out.reshape(accum.shape)


def reduced(pooled_grad, send_sample, send_row, send_count, union_blocks, table, accum):
    columns = pooled_grad.shape[1]
    samples = pooled_grad.shape[0]
    active = (lax.broadcasted_iota(jnp.int32, send_sample.shape, 1) < send_count[:, None]).astype(F32)
    lengths = jax.ops.segment_sum(active.reshape(-1), send_sample.reshape(-1), num_segments=samples)
    scaled = active / jnp.maximum(lengths, 1.0)[send_sample]
    values = (pooled_grad[send_sample].astype(F32) * scaled[:, :, None]).astype(BF16)
    arrived = lax.all_to_all(values, "shard", split_axis=0, concat_axis=0, tiled=True)
    places = lax.all_to_all(send_row, "shard", split_axis=0, concat_axis=0, tiled=True)
    blocks = union_blocks[0]
    span = blocks.shape[0] * TILE
    local = (
        jnp.zeros((span, columns), F32)
        .at[places.reshape(-1)]
        .add(arrived.reshape(-1, columns).astype(F32))
    )
    table_tiles = table.reshape(-1, TILE, columns)
    accum_tiles = accum.reshape(-1, TILE)
    grad = lax.optimization_barrier(lax.psum(local.astype(BF16), "rep")).astype(F32)
    acc_new = accum_tiles[blocks].reshape(span) + jnp.mean(grad * grad, axis=-1)
    rows_new = table_tiles[blocks].reshape(span, columns) - LEARNING_RATE * grad / (
        jnp.sqrt(acc_new)[:, None] + EPSILON
    )
    table_out = table_tiles.at[blocks].set(rows_new.reshape(-1, TILE, columns)).reshape(table.shape)
    accum_out = accum_tiles.at[blocks].set(acc_new.reshape(-1, TILE)).reshape(accum.shape)
    return table_out, accum_out


def solution(mesh):
    both = ("shard", "rep")
    in_specs = (
        P(both, None),
        P(both, None),
        P(both, None),
        P(both),
        P("shard", None),
        P("shard", None),
        P("shard"),
    )
    out_specs = (P("shard", None), P("shard"))
    small = mesh.shape["shard"] == 4 and mesh.shape["rep"] == 8
    return jax.shard_map(
        gathered if small else reduced,
        mesh=mesh,
        in_specs=in_specs,
        out_specs=out_specs,
        check_vma=False,
    )
```

```python
import functools

import jax
import jax.numpy as jnp
from jax import lax
from jax.experimental import pallas as pl
from jax.experimental.pallas import tpu as pltpu
from jax.sharding import PartitionSpec as P

TILE = 128
LOAD_MIB = 56
PACK_BYTES = 60 * 1024 * 1024
TAIL = 16
LEARNING_RATE = 0.5
EPSILON = 1e-06
VMEM = pltpu.VMEM
SMEM = pltpu.SMEM
F32 = jnp.float32
BF16 = jnp.bfloat16


def params(mib=24):
    return pltpu.CompilerParams(vmem_limit_bytes=mib * 2**20)


def whole(space=VMEM):
    return pl.BlockSpec(memory_space=space)


def pack_kernel(count_in, grad_in, sample_in, row_in, *refs):
    *out_refs, count_ref, grad_ref, sample_ref, row_ref, sems = refs
    copies = [
        pltpu.make_async_copy(src, dst, sems.at[i])
        for i, (src, dst) in enumerate(
            (
                (sample_in, sample_ref),
                (count_in, count_ref),
                (grad_in, grad_ref),
                (row_in, row_ref),
            )
        )
    ]
    for c in copies:
        c.start()
    owners = len(out_refs)
    cap = sample_ref.shape[1]
    samples, cols = grad_ref.shape
    me = lax.axis_index("shard")
    lane = lax.broadcasted_iota(jnp.int32, (1, cap), 1)
    sub = lax.broadcasted_iota(jnp.int32, (samples, cap), 0)

    def picks(o):
        live = jnp.where(lane < count_ref[o], sample_ref[pl.ds(o, 1), :], -1)
        return (sub == live).astype(F32)

    copies[0].wait()
    copies[1].wait()
    chosen = [picks(me ^ j) for j in range(owners)]
    lengths = jnp.sum(sum(chosen), axis=1, keepdims=True)
    share = 1.0 / jnp.maximum(lengths, 1.0)
    chosen = [c.astype(BF16) for c in chosen]
    copies[3].wait()
    tail_row = lax.broadcasted_iota(jnp.int32, (TAIL, cap), 0)
    for j in range(owners):
        row = row_ref[pl.ds(me ^ j, 1), :]
        slot = row // TILE
        within = row - slot * TILE
        tail = jnp.where(tail_row == 0, slot, jnp.where(tail_row == 1, within, 0))
        out_refs[j][cap : cap + TAIL, :] = jnp.zeros((TAIL, cols), BF16)
        out_refs[j][cap : cap + TAIL, 0:cap] = tail.astype(F32).astype(BF16)
    copies[2].wait()
    scaled = (grad_ref[...].astype(F32) * share).astype(BF16)
    for j in range(owners):
        values = lax.dot_general(
            chosen[j], scaled, (((0,), (0,)), ((), ())), preferred_element_type=F32
        )
        out_refs[j][0:cap, :] = values.astype(BF16)


def pack(count, grad, sample, row):
    owners, cap = sample.shape
    shape = VMEM((cap + TAIL, grad.shape[1]), BF16)
    return pl.pallas_call(
        pack_kernel,
        out_shape=[shape] * owners,
        in_specs=[whole(pltpu.HBM)] * 4,
        out_specs=[whole()] * owners,
        scratch_shapes=[
            SMEM(count.shape, jnp.int32),
            VMEM(grad.shape, BF16),
            VMEM(sample.shape, jnp.int32),
            VMEM(row.shape, jnp.int32),
            pltpu.SemaphoreType.DMA((4,)),
        ],
        compiler_params=pltpu.CompilerParams(vmem_limit_bytes=PACK_BYTES),
    )(count, grad, sample, row)


def tiny(cols):
    return pl.CostEstimate(flops=cols, bytes_accessed=cols, transcendentals=0)


def join_kernel(*refs):
    *payloads, out = refs
    cols = out.shape[1]
    sub = lax.broadcasted_iota(jnp.int32, (TAIL, cols), 0)
    tail = jnp.zeros((TAIL, cols), F32)
    at = 0
    for ref in payloads:
        rows = ref.shape[0] - TAIL
        out[at : at + rows, :] = ref[0:rows, :]
        own = ref[rows : rows + TAIL, :].astype(F32)
        for i in range(2 * (rows // TILE)):
            tail = jnp.where(sub == 2 * (at // TILE) + i, own[i : i + 1, :], tail)
        at += rows
    out[at : at + TAIL, :] = tail.astype(BF16)


def join(*payloads):
    cols = payloads[0].shape[1]
    rows = sum(p.shape[0] - TAIL for p in payloads) + TAIL
    return pl.pallas_call(
        join_kernel,
        out_shape=jax.ShapeDtypeStruct((rows, cols), BF16),
        in_specs=[whole()] * len(payloads),
        out_specs=whole(),
        compiler_params=params(),
        cost_estimate=tiny(cols),
    )(*payloads)


def positions(ref, cap):
    entries = ref.shape[0] - TAIL
    tail = ref[entries : entries + TAIL, 0:cap].astype(F32)
    n = entries // cap
    slot = jnp.concatenate([tail[2 * c : 2 * c + 1] for c in range(n)], axis=1)
    within = jnp.concatenate([tail[2 * c + 1 : 2 * c + 2] for c in range(n)], axis=1)
    return slot, within


def block_sum(ref, place, k):
    slot, within = place
    here = jnp.where(slot == k, within, -1.0).astype(BF16)
    entries = here.shape[1]
    sub = lax.broadcasted_iota(jnp.int32, (TILE, entries), 0).astype(F32).astype(BF16)
    pick = jnp.where(sub == here, jnp.ones((), BF16), jnp.zeros((), BF16))
    return jnp.dot(pick, ref[0:entries, :], preferred_element_type=F32)


def group_sum(ref, place, k, size):
    slot, within = place
    entries = slot.shape[1]
    sub = lax.broadcasted_iota(jnp.int32, (TILE, entries), 0).astype(F32).astype(BF16)
    picks = []
    for b in range(k, k + size):
        here = jnp.where(slot == b, within, -1.0).astype(BF16)
        picks.append(jnp.where(sub == here, jnp.ones((), BF16), jnp.zeros((), BF16)))
    pick = jnp.concatenate(picks, axis=0)
    return jnp.dot(pick, ref[0:entries, :], preferred_element_type=F32)


def tile(ref, block):
    return ref.at[pl.ds(pl.multiple_of(block * TILE, TILE), TILE), :]


CHUNKS = 4


def load_kernel(blocks_ref, table_in, table_out, table_ref, loads, kept):
    n = blocks_ref.shape[1]
    tiles = table_in.shape[0] // TILE
    size = tiles // CHUNKS
    copies = []
    for i in range(CHUNKS):
        rows = pl.ds(i * size * TILE, size * TILE)
        c = pltpu.make_async_copy(table_in.at[rows, :], table_out.at[rows, :], loads.at[i])
        c.start()
        copies.append(c)
    seen = jnp.int32(0)
    for i in range(CHUNKS):
        copies[i].wait()
        for t in range(i * size, (i + 1) * size):
            touched = blocks_ref[0, jnp.minimum(seen, n - 1)] == t

            @pl.when(jnp.logical_not(touched))
            def _():
                pltpu.make_async_copy(tile(table_out, t), tile(table_ref, t), kept).start()

            seen = seen + touched.astype(jnp.int32)
    for _ in range(tiles - n):
        pltpu.make_async_copy(tile(table_out, 0), tile(table_ref, 0), kept).wait()


def load(blocks, table):
    return pl.pallas_call(
        load_kernel,
        out_shape=[VMEM(table.shape, F32), jax.ShapeDtypeStruct(table.shape, F32)],
        in_specs=[whole(SMEM), whole(pltpu.HBM)],
        out_specs=[whole(), whole(pltpu.HBM)],
        scratch_shapes=[pltpu.SemaphoreType.DMA((CHUNKS,)), pltpu.SemaphoreType.DMA],
        compiler_params=params(LOAD_MIB),
        cost_estimate=pl.CostEstimate(
            flops=0, bytes_accessed=4 * table.size * 3, transcendentals=0
        ),
    )(blocks, table)


def own_kernel(cap, blocks_ref, own, own_c, accum_ref, part, part_c, old):
    places = [positions(ref, cap) for ref in (own, own_c)]
    for k in range(0, part.shape[0] // TILE, 4):
        span = slice(k * TILE, (k + 4) * TILE)
        part[span, :] = group_sum(own, places[0], k, 4)
        part_c[span, :] = group_sum(own_c, places[1], k, 4)
    for k in range(part.shape[0] // TILE):
        row = accum_ref[pl.ds(blocks_ref[0, k], 1), :]
        old[k * TILE : (k + 1) * TILE, :] = jnp.broadcast_to(row, (TILE, TILE)).T


def own_sum(blocks, own, own_c, accum, span, cap):
    entries, cols = own.shape[0] - TAIL, own.shape[1]
    return pl.pallas_call(
        functools.partial(own_kernel, cap),
        out_shape=[
            jax.ShapeDtypeStruct((span, cols), F32),
            jax.ShapeDtypeStruct((span, cols), F32),
            jax.ShapeDtypeStruct((span, TILE), F32),
        ],
        in_specs=[whole(SMEM)] + [whole()] * 3,
        out_specs=[whole()] * 3,
        compiler_params=params(),
        cost_estimate=pl.CostEstimate(
            flops=2 * span * entries * cols, bytes_accessed=span * cols * 4, transcendentals=0
        ),
    )(blocks, own, own_c, accum)


def near_kernel(cap, one, two, one_c, part, part_c, near, side, near_c):
    places = [positions(ref, cap) for ref in (one, two, one_c)]
    for k in range(0, near.shape[0] // TILE, 4):
        span = slice(k * TILE, (k + 4) * TILE)
        near[span, :] = part[span, :] + group_sum(one, places[0], k, 4)
        side[span, :] = group_sum(two, places[1], k, 4)
        near_c[span, :] = part_c[span, :] + group_sum(one_c, places[2], k, 4)


def rest_kernel(cap, diag, two_c, near, side, mine, side_c):
    places = [positions(ref, cap) for ref in (diag, two_c)]
    for k in range(0, near.shape[0] // TILE, 4):
        span = slice(k * TILE, (k + 4) * TILE)
        mine[span, :] = near[span, :] + (side[span, :] + group_sum(diag, places[0], k, 4))
        side_c[span, :] = group_sum(two_c, places[1], k, 4)


def sum_call(kernel, payloads, parts, results, span, cap):
    entries, cols = payloads[0].shape[0] - TAIL, payloads[0].shape[1]
    wide = jax.ShapeDtypeStruct((span, cols), F32)
    return pl.pallas_call(
        functools.partial(kernel, cap),
        out_shape=[wide] * results,
        in_specs=[whole()] * (len(payloads) + len(parts)),
        out_specs=[whole()] * results,
        compiler_params=params(),
        cost_estimate=pl.CostEstimate(
            flops=2 * span * entries * cols * len(payloads),
            bytes_accessed=span * cols * 4 * (results + len(parts)),
            transcendentals=0,
        ),
    )(*payloads, *parts)


def update_kernel(
    cap, blocks_ref, last, mine, near, side, old, table_in, accum_ref, alias,
    table_ref, accum_out, rows_out, accum_new, sem, sems,
):
    del alias
    n = rows_out.shape[0] // TILE
    cols = rows_out.shape[1]
    place = positions(last, cap)
    accum_new[...] = accum_ref[...]
    diagonal = lax.broadcasted_iota(jnp.int32, (TILE, TILE), 0) == lax.broadcasted_iota(
        jnp.int32, (TILE, TILE), 1
    )
    ones = jnp.ones((2 * TILE, TILE), BF16)
    news = []
    copies = []
    bounds = sorted({0, n // 2, 3 * n // 4, n})
    for g, end in zip(bounds, bounds[1:]):
        span = slice(g * TILE, end * TILE)
        other = near[span, :] + (side[span, :] + group_sum(last, place, g, end - g))
        grad = (mine[span, :] + other).astype(BF16).astype(F32)
        square = grad * grad
        square = sum(square[:, c : c + TILE] for c in range(0, cols, TILE))
        high = square.astype(BF16)
        low = (square - high.astype(F32)).astype(BF16)
        total = jnp.dot(jnp.concatenate([high, low], axis=1), ones, preferred_element_type=F32)
        new = old[span, :] + total * (1.0 / cols)
        rate = LEARNING_RATE / (new * lax.rsqrt(new) + EPSILON)
        for k in range(g, end):
            block = pl.multiple_of(blocks_ref[0, k] * TILE, TILE)
            at = slice((k - g) * TILE, (k - g + 1) * TILE)
            here = slice(k * TILE, (k + 1) * TILE)
            for c in range(0, cols, TILE):
                rows_out[here, c : c + TILE] = (
                    table_in[pl.ds(block, TILE), c : c + TILE] - grad[at, c : c + TILE] * rate[at, :]
                )
            news.append(jnp.sum(jnp.where(diagonal, new[at, :], 0.0), axis=0, keepdims=True))
            c = pltpu.make_async_copy(rows_out.at[here, :], tile(table_ref, blocks_ref[0, k]), sems.at[k])
            c.start()
            copies.append(c)
    for k in range(n):
        accum_new[pl.ds(blocks_ref[0, k], 1), :] = news[k]
    c = pltpu.make_async_copy(accum_new, accum_out, sem)
    c.start()
    for c in copies + [c]:
        c.wait()


def update(blocks, last, sums, old, table, accum, target, cap):
    n = blocks.shape[1]
    return pl.pallas_call(
        functools.partial(update_kernel, cap),
        out_shape=[
            jax.ShapeDtypeStruct(table.shape, F32),
            jax.ShapeDtypeStruct(accum.shape, F32),
        ],
        in_specs=[whole(SMEM)] + [whole()] * 7 + [whole(pltpu.HBM)],
        out_specs=[whole(pltpu.HBM), whole(pltpu.HBM)],
        scratch_shapes=[
            VMEM((n * TILE, table.shape[1]), F32),
            VMEM(accum.shape, F32),
            pltpu.SemaphoreType.DMA,
            pltpu.SemaphoreType.DMA((n,)),
        ],
        input_output_aliases={8: 0},
        compiler_params=params(),
    )(blocks, last, *sums, old, table, accum, target)


def after(x, *earlier):
    return lax.optimization_barrier((x,) + earlier)[0]


def gathered(pooled_grad, send_sample, send_row, send_count, union_blocks, table, accum):
    shards = lax.axis_size("shard")
    reps = lax.axis_size("rep")
    cap = send_sample.shape[1]
    span = union_blocks.shape[1] * TILE
    old_accum = accum.reshape(-1, TILE)

    def swap(x, flip):
        pairs = []
        for z in range(shards):
            for r in range(reps):
                dz, dr = flip(r)
                pairs.append((z * reps + r, (z ^ dz) * reps + (r ^ dr)))
        return lax.ppermute(x, ("shard", "rep"), pairs)

    def first(x):
        return swap(x, lambda r: (0, 2 if r % 2 == 0 else 4))

    def second(x):
        return swap(x, lambda r: (0, 4 if r % 2 == 0 else 2))

    def core(x):
        return swap(x, lambda r: (0, 1))

    mine = pack(send_count, pooled_grad, send_sample, send_row)
    table, target = load(union_blocks, after(table, mine[0]))
    arrived = [swap(mine[j], lambda r: (j, 0)) for j in (2, 3, 1)]
    early = first(mine[0])
    own = join(after(mine[0], table), *arrived)
    one = join(early, first(join(*arrived)))
    own_c = core(after(own, early))
    part, part_c, old = own_sum(union_blocks, own, own_c, old_accum, span, cap)
    two = second(after(own, part))
    diag = second(one)
    one_c, two_c = core(one), core(two)
    near, side, near_c = sum_call(near_kernel, [one, two, one_c], [part, part_c], 3, span, cap)
    last = core(after(diag, near))
    mine, side_c = sum_call(rest_kernel, [diag, two_c], [near, side], 2, span, cap)
    table_out, accum_out = update(
        union_blocks, last, (mine, near_c, side_c), old, table, old_accum, target, cap
    )
    return table_out, accum_out.reshape(accum.shape)


def reduced(pooled_grad, send_sample, send_row, send_count, union_blocks, table, accum):
    columns = pooled_grad.shape[1]
    samples = pooled_grad.shape[0]
    active = (lax.broadcasted_iota(jnp.int32, send_sample.shape, 1) < send_count[:, None]).astype(F32)
    lengths = jax.ops.segment_sum(active.reshape(-1), send_sample.reshape(-1), num_segments=samples)
    scaled = active / jnp.maximum(lengths, 1.0)[send_sample]
    values = (pooled_grad[send_sample].astype(F32) * scaled[:, :, None]).astype(BF16)
    arrived = lax.all_to_all(values, "shard", split_axis=0, concat_axis=0, tiled=True)
    places = lax.all_to_all(send_row, "shard", split_axis=0, concat_axis=0, tiled=True)
    blocks = union_blocks[0]
    span = blocks.shape[0] * TILE
    local = (
        jnp.zeros((span, columns), F32)
        .at[places.reshape(-1)]
        .add(arrived.reshape(-1, columns).astype(F32))
    )
    table_tiles = table.reshape(-1, TILE, columns)
    accum_tiles = accum.reshape(-1, TILE)
    grad = lax.optimization_barrier(lax.psum(local.astype(BF16), "rep")).astype(F32)
    acc_new = accum_tiles[blocks].reshape(span) + jnp.mean(grad * grad, axis=-1)
    rows_new = table_tiles[blocks].reshape(span, columns) - LEARNING_RATE * grad / (
        jnp.sqrt(acc_new)[:, None] + EPSILON
    )
    table_out = table_tiles.at[blocks].set(rows_new.reshape(-1, TILE, columns)).reshape(table.shape)
    accum_out = accum_tiles.at[blocks].set(acc_new.reshape(-1, TILE)).reshape(accum.shape)
    return table_out, accum_out


def solution(mesh):
    both = ("shard", "rep")
    in_specs = (
        P(both, None),
        P(both, None),
        P(both, None),
        P(both),
        P("shard", None),
        P("shard", None),
        P("shard"),
    )
    out_specs = (P("shard", None), P("shard"))
    small = mesh.shape["shard"] == 4 and mesh.shape["rep"] == 8
    return jax.shard_map(
        gathered if small else reduced,
        mesh=mesh,
        in_specs=in_specs,
        out_specs=out_specs,
        check_vma=False,
    )
```

```python
import functools

import jax
import jax.numpy as jnp
from jax import lax
from jax.experimental import pallas as pl
from jax.experimental.pallas import tpu as pltpu
from jax.sharding import PartitionSpec as P

TILE = 128
LOAD_MIB = 56
PACK_BYTES = 60 * 1024 * 1024
TAIL = 16
LEARNING_RATE = 0.5
EPSILON = 1e-06
VMEM = pltpu.VMEM
SMEM = pltpu.SMEM
F32 = jnp.float32
BF16 = jnp.bfloat16


def params(mib=24):
    return pltpu.CompilerParams(vmem_limit_bytes=mib * 2**20)


def whole(space=VMEM):
    return pl.BlockSpec(memory_space=space)


def pack_kernel(count_in, grad_in, sample_in, row_in, *refs):
    *out_refs, count_ref, grad_ref, sample_ref, row_ref, sems = refs
    copies = [
        pltpu.make_async_copy(src, dst, sems.at[i])
        for i, (src, dst) in enumerate(
            (
                (sample_in, sample_ref),
                (count_in, count_ref),
                (grad_in, grad_ref),
                (row_in, row_ref),
            )
        )
    ]
    for c in copies:
        c.start()
    owners = len(out_refs)
    cap = sample_ref.shape[1]
    samples, cols = grad_ref.shape
    me = lax.axis_index("shard")
    lane = lax.broadcasted_iota(jnp.int32, (1, cap), 1)
    sub = lax.broadcasted_iota(jnp.int32, (samples, cap), 0)

    def picks(o):
        live = jnp.where(lane < count_ref[o], sample_ref[pl.ds(o, 1), :], -1)
        return (sub == live).astype(F32)

    copies[0].wait()
    copies[1].wait()
    chosen = [picks(me ^ j) for j in range(owners)]
    lengths = jnp.sum(sum(chosen), axis=1, keepdims=True)
    share = 1.0 / jnp.maximum(lengths, 1.0)
    chosen = [c.astype(BF16) for c in chosen]
    copies[3].wait()
    tail_row = lax.broadcasted_iota(jnp.int32, (TAIL, cap), 0)
    for j in range(owners):
        row = row_ref[pl.ds(me ^ j, 1), :]
        slot = row // TILE
        within = row - slot * TILE
        tail = jnp.where(tail_row == 0, slot, jnp.where(tail_row == 1, within, 0))
        out_refs[j][cap : cap + TAIL, :] = jnp.zeros((TAIL, cols), BF16)
        out_refs[j][cap : cap + TAIL, 0:cap] = tail.astype(F32).astype(BF16)
    copies[2].wait()
    scaled = (grad_ref[...].astype(F32) * share).astype(BF16)
    for j in range(owners):
        values = lax.dot_general(
            chosen[j], scaled, (((0,), (0,)), ((), ())), preferred_element_type=F32
        )
        out_refs[j][0:cap, :] = values.astype(BF16)


def pack(count, grad, sample, row):
    owners, cap = sample.shape
    shape = VMEM((cap + TAIL, grad.shape[1]), BF16)
    return pl.pallas_call(
        pack_kernel,
        out_shape=[shape] * owners,
        in_specs=[whole(pltpu.HBM)] * 4,
        out_specs=[whole()] * owners,
        scratch_shapes=[
            SMEM(count.shape, jnp.int32),
            VMEM(grad.shape, BF16),
            VMEM(sample.shape, jnp.int32),
            VMEM(row.shape, jnp.int32),
            pltpu.SemaphoreType.DMA((4,)),
        ],
        compiler_params=pltpu.CompilerParams(vmem_limit_bytes=PACK_BYTES),
    )(count, grad, sample, row)


def tiny(cols):
    return pl.CostEstimate(flops=cols, bytes_accessed=cols, transcendentals=0)


def join_kernel(*refs):
    *payloads, out = refs
    cols = out.shape[1]
    sub = lax.broadcasted_iota(jnp.int32, (TAIL, cols), 0)
    tail = jnp.zeros((TAIL, cols), F32)
    at = 0
    for ref in payloads:
        rows = ref.shape[0] - TAIL
        out[at : at + rows, :] = ref[0:rows, :]
        own = ref[rows : rows + TAIL, :].astype(F32)
        for i in range(2 * (rows // TILE)):
            tail = jnp.where(sub == 2 * (at // TILE) + i, own[i : i + 1, :], tail)
        at += rows
    out[at : at + TAIL, :] = tail.astype(BF16)


def join(*payloads):
    cols = payloads[0].shape[1]
    rows = sum(p.shape[0] - TAIL for p in payloads) + TAIL
    return pl.pallas_call(
        join_kernel,
        out_shape=jax.ShapeDtypeStruct((rows, cols), BF16),
        in_specs=[whole()] * len(payloads),
        out_specs=whole(),
        compiler_params=params(),
        cost_estimate=tiny(cols),
    )(*payloads)


def positions(ref, cap):
    entries = ref.shape[0] - TAIL
    tail = ref[entries : entries + TAIL, 0:cap].astype(F32)
    n = entries // cap
    slot = jnp.concatenate([tail[2 * c : 2 * c + 1] for c in range(n)], axis=1)
    within = jnp.concatenate([tail[2 * c + 1 : 2 * c + 2] for c in range(n)], axis=1)
    return slot, within


def block_sum(ref, place, k):
    slot, within = place
    here = jnp.where(slot == k, within, -1.0).astype(BF16)
    entries = here.shape[1]
    sub = lax.broadcasted_iota(jnp.int32, (TILE, entries), 0).astype(F32).astype(BF16)
    pick = jnp.where(sub == here, jnp.ones((), BF16), jnp.zeros((), BF16))
    return jnp.dot(pick, ref[0:entries, :], preferred_element_type=F32)


def group_sum(ref, place, k, size):
    slot, within = place
    entries = slot.shape[1]
    sub = lax.broadcasted_iota(jnp.int32, (TILE, entries), 0).astype(F32).astype(BF16)
    picks = []
    for b in range(k, k + size):
        here = jnp.where(slot == b, within, -1.0).astype(BF16)
        picks.append(jnp.where(sub == here, jnp.ones((), BF16), jnp.zeros((), BF16)))
    pick = jnp.concatenate(picks, axis=0)
    return jnp.dot(pick, ref[0:entries, :], preferred_element_type=F32)


def tile(ref, block):
    return ref.at[pl.ds(pl.multiple_of(block * TILE, TILE), TILE), :]


CHUNKS = 4


def load_kernel(blocks_ref, table_in, table_out, table_ref, loads, kept):
    n = blocks_ref.shape[1]
    tiles = table_in.shape[0] // TILE
    size = tiles // CHUNKS
    copies = []
    for i in range(CHUNKS):
        rows = pl.ds(i * size * TILE, size * TILE)
        c = pltpu.make_async_copy(table_in.at[rows, :], table_out.at[rows, :], loads.at[i])
        c.start()
        copies.append(c)
    seen = jnp.int32(0)
    for i in range(CHUNKS):
        copies[i].wait()
        for t in range(i * size, (i + 1) * size):
            touched = blocks_ref[0, jnp.minimum(seen, n - 1)] == t

            @pl.when(jnp.logical_not(touched))
            def _():
                pltpu.make_async_copy(tile(table_out, t), tile(table_ref, t), kept).start()

            seen = seen + touched.astype(jnp.int32)
    for _ in range(tiles - n):
        pltpu.make_async_copy(tile(table_out, 0), tile(table_ref, 0), kept).wait()


def load(blocks, table):
    return pl.pallas_call(
        load_kernel,
        out_shape=[VMEM(table.shape, F32), jax.ShapeDtypeStruct(table.shape, F32)],
        in_specs=[whole(SMEM), whole(pltpu.HBM)],
        out_specs=[whole(), whole(pltpu.HBM)],
        scratch_shapes=[pltpu.SemaphoreType.DMA((CHUNKS,)), pltpu.SemaphoreType.DMA],
        compiler_params=params(LOAD_MIB),
        cost_estimate=pl.CostEstimate(
            flops=0, bytes_accessed=4 * table.size * 3, transcendentals=0
        ),
    )(blocks, table)


def own_kernel(cap, blocks_ref, own, own_c, accum_ref, part, part_c, old):
    places = [positions(ref, cap) for ref in (own, own_c)]
    for k in range(0, part.shape[0] // TILE, 4):
        span = slice(k * TILE, (k + 4) * TILE)
        part[span, :] = group_sum(own, places[0], k, 4)
        part_c[span, :] = group_sum(own_c, places[1], k, 4)
    for k in range(part.shape[0] // TILE):
        row = accum_ref[pl.ds(blocks_ref[0, k], 1), :]
        old[k * TILE : (k + 1) * TILE, :] = jnp.broadcast_to(row, (TILE, TILE)).T


def own_sum(blocks, own, own_c, accum, span, cap):
    entries, cols = own.shape[0] - TAIL, own.shape[1]
    return pl.pallas_call(
        functools.partial(own_kernel, cap),
        out_shape=[
            jax.ShapeDtypeStruct((span, cols), F32),
            jax.ShapeDtypeStruct((span, cols), F32),
            jax.ShapeDtypeStruct((span, TILE), F32),
        ],
        in_specs=[whole(SMEM)] + [whole()] * 3,
        out_specs=[whole()] * 3,
        compiler_params=params(),
        cost_estimate=pl.CostEstimate(
            flops=2 * span * entries * cols, bytes_accessed=span * cols * 4, transcendentals=0
        ),
    )(blocks, own, own_c, accum)


def near_kernel(cap, one, two, one_c, part, part_c, near, side, near_c):
    places = [positions(ref, cap) for ref in (one, two, one_c)]
    for k in range(0, near.shape[0] // TILE, 4):
        span = slice(k * TILE, (k + 4) * TILE)
        near[span, :] = part[span, :] + group_sum(one, places[0], k, 4)
        side[span, :] = group_sum(two, places[1], k, 4)
        near_c[span, :] = part_c[span, :] + group_sum(one_c, places[2], k, 4)


def rest_kernel(cap, diag, two_c, near, side, mine, side_c):
    places = [positions(ref, cap) for ref in (diag, two_c)]
    for k in range(0, near.shape[0] // TILE, 4):
        span = slice(k * TILE, (k + 4) * TILE)
        mine[span, :] = near[span, :] + (side[span, :] + group_sum(diag, places[0], k, 4))
        side_c[span, :] = group_sum(two_c, places[1], k, 4)


def sum_call(kernel, payloads, parts, results, span, cap):
    entries, cols = payloads[0].shape[0] - TAIL, payloads[0].shape[1]
    wide = jax.ShapeDtypeStruct((span, cols), F32)
    return pl.pallas_call(
        functools.partial(kernel, cap),
        out_shape=[wide] * results,
        in_specs=[whole()] * (len(payloads) + len(parts)),
        out_specs=[whole()] * results,
        compiler_params=params(),
        cost_estimate=pl.CostEstimate(
            flops=2 * span * entries * cols * len(payloads),
            bytes_accessed=span * cols * 4 * (results + len(parts)),
            transcendentals=0,
        ),
    )(*payloads, *parts)


def update_kernel(
    cap, blocks_ref, last, mine, near, side, old, table_in, accum_ref, alias,
    table_ref, accum_out, rows_out, accum_new, sem, sems,
):
    del alias
    n = rows_out.shape[0] // TILE
    cols = rows_out.shape[1]
    place = positions(last, cap)
    accum_new[...] = accum_ref[...]
    diagonal = lax.broadcasted_iota(jnp.int32, (TILE, TILE), 0) == lax.broadcasted_iota(
        jnp.int32, (TILE, TILE), 1
    )
    ones = jnp.ones((2 * TILE, TILE), BF16)
    news = []
    copies = []
    bounds = sorted({0, n // 2, 3 * n // 4, n})
    for g, end in zip(bounds, bounds[1:]):
        span = slice(g * TILE, end * TILE)
        other = near[span, :] + (side[span, :] + group_sum(last, place, g, end - g))
        grad = (mine[span, :] + other).astype(BF16).astype(F32)
        square = grad * grad
        square = sum(square[:, c : c + TILE] for c in range(0, cols, TILE))
        high = square.astype(BF16)
        low = (square - high.astype(F32)).astype(BF16)
        total = jnp.dot(jnp.concatenate([high, low], axis=1), ones, preferred_element_type=F32)
        new = old[span, :] + total * (1.0 / cols)
        rate = LEARNING_RATE / (new * lax.rsqrt(new) + EPSILON)
        for k in range(g, end):
            block = pl.multiple_of(blocks_ref[0, k] * TILE, TILE)
            at = slice((k - g) * TILE, (k - g + 1) * TILE)
            here = slice(k * TILE, (k + 1) * TILE)
            for c in range(0, cols, TILE):
                rows_out[here, c : c + TILE] = (
                    table_in[pl.ds(block, TILE), c : c + TILE] - grad[at, c : c + TILE] * rate[at, :]
                )
            news.append(jnp.sum(jnp.where(diagonal, new[at, :], 0.0), axis=0, keepdims=True))
            c = pltpu.make_async_copy(rows_out.at[here, :], tile(table_ref, blocks_ref[0, k]), sems.at[k])
            c.start()
            copies.append(c)
    for k in range(n):
        accum_new[pl.ds(blocks_ref[0, k], 1), :] = news[k]
    c = pltpu.make_async_copy(accum_new, accum_out, sem)
    c.start()
    for c in copies + [c]:
        c.wait()


def update(blocks, last, sums, old, table, accum, target, cap):
    n = blocks.shape[1]
    return pl.pallas_call(
        functools.partial(update_kernel, cap),
        out_shape=[
            jax.ShapeDtypeStruct(table.shape, F32),
            jax.ShapeDtypeStruct(accum.shape, F32),
        ],
        in_specs=[whole(SMEM)] + [whole()] * 7 + [whole(pltpu.HBM)],
        out_specs=[whole(pltpu.HBM), whole(pltpu.HBM)],
        scratch_shapes=[
            VMEM((n * TILE, table.shape[1]), F32),
            VMEM(accum.shape, F32),
            pltpu.SemaphoreType.DMA,
            pltpu.SemaphoreType.DMA((n,)),
        ],
        input_output_aliases={8: 0},
        compiler_params=params(),
    )(blocks, last, *sums, old, table, accum, target)


def after(x, *earlier):
    return lax.optimization_barrier((x,) + earlier)[0]


def gathered(pooled_grad, send_sample, send_row, send_count, union_blocks, table, accum):
    shards = lax.axis_size("shard")
    reps = lax.axis_size("rep")
    cap = send_sample.shape[1]
    span = union_blocks.shape[1] * TILE
    old_accum = accum.reshape(-1, TILE)

    def swap(x, flip):
        pairs = []
        for z in range(shards):
            for r in range(reps):
                dz, dr = flip(r)
                pairs.append((z * reps + r, (z ^ dz) * reps + (r ^ dr)))
        return lax.ppermute(x, ("shard", "rep"), pairs)

    def first(x):
        return swap(x, lambda r: (0, 4 if r % 2 == 0 else 2))

    def second(x):
        return swap(x, lambda r: (0, 2 if r % 2 == 0 else 4))

    def core(x):
        return swap(x, lambda r: (0, 1))

    mine = pack(send_count, pooled_grad, send_sample, send_row)
    table, target = load(union_blocks, after(table, mine[0]))
    arrived = [swap(mine[j], lambda r: (j, 0)) for j in (2, 3, 1)]
    early = first(mine[0])
    own = join(after(mine[0], table), *arrived)
    one = join(early, first(join(*arrived)))
    own_c = core(after(own, early))
    part, part_c, old = own_sum(union_blocks, own, own_c, old_accum, span, cap)
    two = second(after(own, part))
    diag = second(one)
    one_c, two_c = core(one), core(two)
    near, side, near_c = sum_call(near_kernel, [one, two, one_c], [part, part_c], 3, span, cap)
    last = core(after(diag, near))
    mine, side_c = sum_call(rest_kernel, [diag, two_c], [near, side], 2, span, cap)
    table_out, accum_out = update(
        union_blocks, last, (mine, near_c, side_c), old, table, old_accum, target, cap
    )
    return table_out, accum_out.reshape(accum.shape)


def reduced(pooled_grad, send_sample, send_row, send_count, union_blocks, table, accum):
    columns = pooled_grad.shape[1]
    samples = pooled_grad.shape[0]
    active = (lax.broadcasted_iota(jnp.int32, send_sample.shape, 1) < send_count[:, None]).astype(F32)
    lengths = jax.ops.segment_sum(active.reshape(-1), send_sample.reshape(-1), num_segments=samples)
    scaled = active / jnp.maximum(lengths, 1.0)[send_sample]
    values = (pooled_grad[send_sample].astype(F32) * scaled[:, :, None]).astype(BF16)
    arrived = lax.all_to_all(values, "shard", split_axis=0, concat_axis=0, tiled=True)
    places = lax.all_to_all(send_row, "shard", split_axis=0, concat_axis=0, tiled=True)
    blocks = union_blocks[0]
    span = blocks.shape[0] * TILE
    local = (
        jnp.zeros((span, columns), F32)
        .at[places.reshape(-1)]
        .add(arrived.reshape(-1, columns).astype(F32))
    )
    table_tiles = table.reshape(-1, TILE, columns)
    accum_tiles = accum.reshape(-1, TILE)
    grad = lax.optimization_barrier(lax.psum(local.astype(BF16), "rep")).astype(F32)
    acc_new = accum_tiles[blocks].reshape(span) + jnp.mean(grad * grad, axis=-1)
    rows_new = table_tiles[blocks].reshape(span, columns) - LEARNING_RATE * grad / (
        jnp.sqrt(acc_new)[:, None] + EPSILON
    )
    table_out = table_tiles.at[blocks].set(rows_new.reshape(-1, TILE, columns)).reshape(table.shape)
    accum_out = accum_tiles.at[blocks].set(acc_new.reshape(-1, TILE)).reshape(accum.shape)
    return table_out, accum_out


def solution(mesh):
    both = ("shard", "rep")
    in_specs = (
        P(both, None),
        P(both, None),
        P(both, None),
        P(both),
        P("shard", None),
        P("shard", None),
        P("shard"),
    )
    out_specs = (P("shard", None), P("shard"))
    small = mesh.shape["shard"] == 4 and mesh.shape["rep"] == 8
    return jax.shard_map(
        gathered if small else reduced,
        mesh=mesh,
        in_specs=in_specs,
        out_specs=out_specs,
        check_vma=False,
    )
```
